32 devices in a mesh: ctx: 8 (over z, x), exp: 4 (over y, core).
Axes of the slice: x: 2, y: 2, z: 4, core: 2. Of those that a mesh axis runs over, the one named last changes fastest.
Arguments:
- residual: bfloat16 [4, 1024, 2048], P('exp', 'ctx'), may hold values from -6 to 6
- query_heads: bfloat16 [4, 1024, 2048], P('exp', 'ctx'), may hold values from -6.5 to 6.5
- key_heads: bfloat16 [4, 1024, 256], P('exp', 'ctx'), may hold values from -6 to 6
- value_heads: bfloat16 [4, 1024, 256], P('exp', 'ctx'), may hold values from -6 to 6
- norm_gain: float32 [2048], replicated, may hold values from 0.1 to 1.9
- chosen_experts: int32 [4, 1024, 8], P('exp', 'ctx'), may hold values from 0 to 31, all different within a row; in each aligned block of 128 rows (0 to 127, 128 to 255, ..., all dimensions but the last counted through in order) at most 36 rows name the same one
- route_weights: float32 [4, 1024, 8], P('exp', 'ctx'), may hold values from 0.05 to 1
- gate_weight: bfloat16 [32, 2048, 768], P(('ctx', 'exp')), may hold values from -0.125 to 0.125
- up_weight: bfloat16 [32, 2048, 768], P(('ctx', 'exp')), may hold values from -0.125 to 0.125
- down_weight: bfloat16 [32, 768, 2048], P(('ctx', 'exp')), may hold values from -0.21875 to 0.21875
- cotangent: bfloat16 [4, 1024, 2048], P('exp', 'ctx'), may hold values from -6 to 6
Outputs:
- layer_out: bfloat16 [4, 1024, 2048], P('exp', 'ctx')
- residual_gradient: bfloat16 [4, 1024, 2048], P('exp', 'ctx')
- query_gradient: bfloat16 [4, 1024, 2048], P('exp', 'ctx')
- key_gradient: bfloat16 [4, 1024, 256], P('exp', 'ctx')
- value_gradient: bfloat16 [4, 1024, 256], P('exp', 'ctx')
- route_gradient: float32 [4, 1024, 8], P('exp', 'ctx')
The draws below stay inside these ranges and needn't reach their ends.
Inputs may be any that keep to these rules, and one draw needn't show every extreme that they name: `chosen_experts`: among the rows of one device no expert is named by more than 36 rows, a bound that some block reaches; the 8 experts of a row differ.
All inputs are finite; a program needn't handle non-finite values.
Results may differ from the reference program's by a relative error of at most 0.025.
Values may be sent and summed in bfloat16 or wider, within the bound.
No kernel may reach another device: no remote copies, remote signals or barrier semaphores. Data moves between devices by JAX's collectives and lax.ppermute only.
A program may use at most 192 MiB of HBM per device.

```python
import math
import jax
import jax.numpy as jnp
import numpy as np
from jax import lax

D = 2048
H = 16
KVH = 2
DH = 128
F = 768
TOPK = 8
TOK_DEV = 128
EXPERTS = 32
SEQ = 1024
SEQS = 4
CAP = 36


def draw_query_heads(key, part):
    drawn_base = jnp.clip(jax.random.normal(jax.random.fold_in(key, 11), (SEQS, SEQ, H * DH), jnp.float32), -6.0, 6.0)
    return drawn_base.astype(jnp.bfloat16)


def draw_key_heads(key, part):
    drawn_base = jnp.clip(jax.random.normal(jax.random.fold_in(key, 12), (SEQS, SEQ, KVH * DH), jnp.float32), -6.0, 6.0)
    return drawn_base.astype(jnp.bfloat16)


def steps_of(key, shape, split, least, high):
    def one(dim, shards_of):
        steps = jax.random.uniform(jax.random.fold_in(jax.random.fold_in(key, 6), dim), (shards_of,), jnp.float32, least / len(split), high / len(split))
        return jnp.repeat(jnp.exp(steps), shape[dim] // shards_of).reshape((-1,) + (1,) * (len(shape) - dim - 1))

    factor_of = one(*split[0])
    for cut in split[1:]:
        factor_of = factor_of * one(*cut)
    return factor_of


def routed_block(own_key, own, number, rows, number_of, top, limit, slope):
    sequence = jax.random.permutation(own_key, number_of)
    heavy_load, usual = portions_of(number_of, rows * top, limit, slope, True), portions_of(number_of, rows * top, limit, slope, False)
    places = jnp.arange(number_of)

    def named(lengths, rotation):
        used = int((lengths > 0).sum())
        fixed = max(1, used // 4)
        shifted = fixed + (places - fixed + rotation * (used - fixed)) % max(1, number_of - fixed)
        return jnp.zeros((number_of,), jnp.int32).at[sequence[jnp.where(places < fixed, places, shifted)]].set(jnp.asarray(lengths, jnp.int32))

    lengths = jnp.where(number % 4 == 0, named(heavy_load, number // 4), named(usual, number - number // 4 - 1))
    mixed = jax.random.permutation(jax.random.fold_in(own, 3), number_of)
    source_of, taker = mixed[0:number_of // 2 * 2:2], mixed[1:number_of // 2 * 2:2]
    margin = jnp.minimum(lengths[source_of] - 1, limit - lengths[taker]) // 2
    margin = jnp.where((source_of == sequence[0]) | (taker == sequence[0]) | (lengths[taker] == 0), 0, jnp.maximum(margin, 0))
    shifted = jax.random.randint(jax.random.fold_in(own, 4), (number_of // 2,), 0, 1 << 20) % (margin + 1)
    lengths = lengths.at[source_of].add(-shifted).at[taker].add(shifted)
    labels = jnp.searchsorted(jnp.cumsum(lengths), jnp.arange(rows * top), side="right").astype(jnp.int32)
    table = labels.reshape(top, rows).T
    table = table[jax.random.permutation(jax.random.fold_in(own, 1), rows)]
    rotation = jax.random.randint(jax.random.fold_in(own, 2), (rows, 1), 0, top)
    return jnp.take_along_axis(table, (jnp.arange(top)[None, :] + rotation) % top, axis=1)


def portions_of(count, total, limit, skew, full):
    portions = [(1 << 20) // math.isqrt(grade ** skew) + 1 for grade in range(1, count + 1)]
    largest = limit if full else min(limit, max(-(-total // count), total * portions[0] // sum(portions)))
    least = 1 if total - largest >= count - 1 else 0
    counts, rest = [largest] + [least] * (count - 1), total - largest - least * (count - 1)
    while rest > 0:
        candidates = [i for i in range(1, count) if counts[i] < largest] or [i for i in range(1, count) if counts[i] < limit]
        whole, left = sum([portions[i] for i in candidates]), rest
        for i in candidates:
            extra = min(limit - counts[i], max(1, left * portions[i] // whole), rest)
            counts[i] = counts[i] + extra
            rest = rest - extra
    return np.array(counts)


def gaussian(rng, dims, deviation, limit, split=(), kind=jnp.bfloat16):
    values = deviation * jax.random.normal(rng, dims, jnp.float32)
    if split:
        values = values * steps_of(rng, dims, split, -0.22, 0.18)
    return jnp.clip(values, -limit, limit).astype(kind)


def setup_inputs(seed: int = 0) -> dict:
    arg_keys = jax.random.split(jax.random.key(seed), 12)
    residual = gaussian(arg_keys[0], (SEQS, SEQ, D), 1.0, 6.0, ((0, 4), (1, 8)))
    query_heads = draw_query_heads(jax.random.fold_in(arg_keys[11], 71), 0)
    key_heads = draw_key_heads(jax.random.fold_in(arg_keys[11], 71), 0)
    value_heads = gaussian(arg_keys[3], (SEQS, SEQ, KVH * DH), 1.0, 6.0, ((0, 4), (1, 8)))
    norm_gain = jnp.clip(1.0 + 0.18 * jax.random.normal(arg_keys[4], (D,), jnp.float32), 0.1, 1.9)
    chosen_experts_keys = jax.random.split(jax.random.fold_in(arg_keys[5], 1), SEQS * SEQ // TOK_DEV)
    chosen_experts_turns = jax.random.permutation(jax.random.fold_in(arg_keys[5], 3), SEQS * SEQ // TOK_DEV)
    chosen_experts = jax.vmap(lambda own, number: routed_block(jax.random.fold_in(arg_keys[5], 2), own, number, TOK_DEV, EXPERTS, TOPK, CAP, 0))(chosen_experts_keys, chosen_experts_turns).reshape((SEQS, SEQ, TOPK))
    route_weights = jnp.clip(jnp.exp(math.log(1.0) - 2.9957323 * jax.random.uniform(arg_keys[6], (SEQS, SEQ, TOPK), jnp.float32) ** steps_of(arg_keys[6], (SEQS, SEQ, TOPK), ((0, 4), (1, 8)), -0.2, 0.2)), 0.05, 1.0)
    gate_weight = gaussian(arg_keys[7], (EXPERTS, D, F), D ** -0.5, 0.125, ((0, 32),))
    up_weight = gaussian(arg_keys[8], (EXPERTS, D, F), D ** -0.5, 0.125, ((0, 32),))
    down_weight = gaussian(arg_keys[9], (EXPERTS, F, D), F ** -0.5, 0.21875, ((0, 32),))
    cotangent = gaussian(arg_keys[10], (SEQS, SEQ, D), 1.0, 6.0, ((0, 4), (1, 8)))
    return {"residual": residual, "query_heads": query_heads, "key_heads": key_heads, "value_heads": value_heads, "norm_gain": norm_gain, "chosen_experts": chosen_experts, "route_weights": route_weights, "gate_weight": gate_weight, "up_weight": up_weight, "down_weight": down_weight, "cotangent": cotangent}


NEG = -1e+30
EPSILON = 1e-06

def to_bfloat(values):
    return lax.optimization_barrier(values.astype(jnp.bfloat16)).astype(jnp.float32)

def attend_forward(query_seq, key_seq, value_seq):
    score_scale = DH ** (-0.5)
    block_rows = min(512, SEQ)
    out_parts = []
    log_parts = []
    for begin_row in range(0, SEQ, block_rows):
        end_row = begin_row + block_rows
        scores = jnp.einsum('ikgd,jkd->kgij', query_seq[begin_row:end_row], key_seq[:end_row]) * score_scale
        allowed = jnp.arange(end_row)[None, :] <= jnp.arange(begin_row, end_row)[:, None]
        scores = jnp.where(allowed, scores, NEG)
        row_max = lax.optimization_barrier(jnp.max(scores, axis=-1, keepdims=True))
        weights = jnp.where(allowed, jnp.exp(scores - row_max), 0.0)
        row_sum = lax.optimization_barrier(jnp.sum(weights, axis=-1, keepdims=True))
        mixed_part = jnp.einsum('kgij,jkd->kgid', to_bfloat(weights), value_seq[:end_row]) / row_sum
        out_parts.append(mixed_part)
        log_parts.append((row_max + jnp.log(row_sum))[..., 0])
    attended = jnp.concatenate(out_parts, axis=2)
    attended = jnp.transpose(attended, (2, 0, 1, 3)).reshape(SEQ, H * DH).astype(jnp.bfloat16)
    return (attended, jnp.concatenate(log_parts, axis=2))

def attend_backward(query_seq, key_seq, value_seq, attended, grad_out, log_sum):
    score_scale = DH ** (-0.5)
    block_rows = min(512, SEQ)
    row_dot = jnp.einsum('ikgd,ikgd->kgi', grad_out, attended)
    key_grad = jnp.zeros((SEQ, KVH, DH), jnp.float32)
    value_grad = jnp.zeros((SEQ, KVH, DH), jnp.float32)
    query_parts = []
    for begin_row in range(0, SEQ, block_rows):
        end_row = begin_row + block_rows
        query_part = query_seq[begin_row:end_row]
        grad_part = grad_out[begin_row:end_row]
        scores = jnp.einsum('ikgd,jkd->kgij', query_part, key_seq[:end_row]) * score_scale
        allowed = jnp.arange(end_row)[None, :] <= jnp.arange(begin_row, end_row)[:, None]
        weights = jnp.where(allowed, jnp.exp(scores - log_sum[:, :, begin_row:end_row, None]), 0.0)
        value_grad = value_grad.at[:end_row].add(jnp.einsum('kgij,ikgd->jkd', to_bfloat(weights), grad_part))
        grad_weights = jnp.einsum('ikgd,jkd->kgij', grad_part, value_seq[:end_row])
        grad_scores = to_bfloat(weights * (grad_weights - row_dot[:, :, begin_row:end_row, None]))
        query_parts.append(jnp.einsum('kgij,jkd->ikgd', grad_scores, key_seq[:end_row]) * score_scale)
        key_grad = key_grad.at[:end_row].add(jnp.einsum('kgij,ikgd->jkd', grad_scores, query_part) * score_scale)
    query_grad = jnp.concatenate(query_parts, axis=0).reshape(SEQ, H * DH).astype(jnp.bfloat16)
    return (query_grad, key_grad.reshape(SEQ, KVH * DH).astype(jnp.bfloat16), value_grad.reshape(SEQ, KVH * DH).astype(jnp.bfloat16))

def reference(residual, query_heads, key_heads, value_heads, norm_gain, chosen_experts, route_weights, gate_weight, up_weight, down_weight, cotangent):
    group_size = H // KVH
    tokens_all = SEQS * SEQ
    hidden_list = []
    saved = []
    for seq_index in range(SEQS):
        query_seq = query_heads[seq_index].astype(jnp.float32).reshape(SEQ, KVH, group_size, DH)
        key_seq = key_heads[seq_index].astype(jnp.float32).reshape(SEQ, KVH, DH)
        value_seq = value_heads[seq_index].astype(jnp.float32).reshape(SEQ, KVH, DH)
        attended, log_sum = attend_forward(query_seq, key_seq, value_seq)
        saved.append((query_seq, key_seq, value_seq, attended, log_sum))
        hidden_list.append((residual[seq_index].astype(jnp.float32) + attended.astype(jnp.float32)).astype(jnp.bfloat16))
    hidden = jnp.concatenate(hidden_list, axis=0)
    hidden_float = hidden.astype(jnp.float32)
    inverse = lax.rsqrt(lax.optimization_barrier(jnp.mean(hidden_float * hidden_float, axis=-1, keepdims=True)) + EPSILON)
    normed = (hidden_float * inverse * norm_gain).astype(jnp.bfloat16)
    chosen_flat = chosen_experts.reshape(-1).astype(jnp.int32)
    share_raw = route_weights.reshape(tokens_all, TOPK)
    route_total = lax.optimization_barrier(jnp.sum(share_raw, axis=-1, keepdims=True))
    route_share = share_raw / route_total
    share_flat = route_share.reshape(-1)
    cot_float = cotangent.reshape(tokens_all, D).astype(jnp.float32)
    assignments = tokens_all * TOPK
    slots_each = EXPERTS * CAP
    onehot_hits = (chosen_flat[:, None] == jnp.arange(EXPERTS, dtype=jnp.int32)[None, :]).astype(jnp.int32)
    earlier = jnp.cumsum(onehot_hits, axis=0) - onehot_hits
    slot_index = lax.optimization_barrier(jnp.sum(earlier * onehot_hits, axis=1)).astype(jnp.int32)
    table = jnp.full((EXPERTS, slots_each), -1, jnp.int32).at[chosen_flat, slot_index].set(jnp.arange(assignments, dtype=jnp.int32))

    def expert_rows(slot_ids):
        is_filled = slot_ids >= 0
        assign = jnp.maximum(slot_ids, 0)
        token_ids = assign // TOPK
        row_inputs = jnp.where(is_filled[:, None], normed[token_ids], jnp.zeros((), jnp.bfloat16))
        return (is_filled, assign, token_ids, row_inputs)

    def expert_forward(carry, stacked):
        moe_sum, route_dot = carry
        slot_ids, gate_mat, up_mat, down_mat = stacked
        is_filled, assign, token_ids, row_inputs = expert_rows(slot_ids)
        gate_act = jnp.dot(row_inputs, gate_mat, preferred_element_type=jnp.float32)
        up_act = jnp.dot(row_inputs, up_mat, preferred_element_type=jnp.float32)
        activation = (jax.nn.silu(gate_act) * up_act).astype(jnp.bfloat16)
        produced = to_bfloat(jnp.dot(activation, down_mat, preferred_element_type=jnp.float32))
        produced = jnp.where(is_filled[:, None], produced, 0.0)
        moe_sum = moe_sum.at[token_ids].add(share_flat[assign][:, None] * produced)
        route_dot = route_dot.at[assign].add(lax.optimization_barrier(jnp.sum(produced * cot_float[token_ids], axis=-1)))
        return ((moe_sum, route_dot), None)

    def expert_backward(carry, stacked):
        slot_ids, gate_mat, up_mat, down_mat = stacked
        is_filled, assign, token_ids, row_inputs = expert_rows(slot_ids)
        gate_act = jnp.dot(row_inputs, gate_mat, preferred_element_type=jnp.float32)
        up_act = jnp.dot(row_inputs, up_mat, preferred_element_type=jnp.float32)
        out_cot = jnp.where(is_filled[:, None], share_flat[assign][:, None] * cot_float[token_ids], 0.0).astype(jnp.bfloat16)
        act_cot = jnp.dot(out_cot, down_mat.T, preferred_element_type=jnp.float32)
        sigma_gate = jax.nn.sigmoid(gate_act)
        gate_cot = (act_cot * up_act * sigma_gate * (1.0 + gate_act * (1.0 - sigma_gate))).astype(jnp.bfloat16)
        up_cot = (act_cot * gate_act * sigma_gate).astype(jnp.bfloat16)
        row_cot = to_bfloat(jnp.dot(gate_cot, gate_mat.T, preferred_element_type=jnp.float32) + jnp.dot(up_cot, up_mat.T, preferred_element_type=jnp.float32))
        carry = carry.at[token_ids].add(jnp.where(is_filled[:, None], row_cot, 0.0))
        return (carry, None)
    stacked_all = (table, gate_weight, up_weight, down_weight)
    (moe_sum, route_dot), unused = lax.scan(expert_forward, (jnp.zeros((tokens_all, D), jnp.float32), jnp.zeros((assignments,), jnp.float32)), stacked_all)
    layer_out = (hidden_float + moe_sum).astype(jnp.bfloat16)
    route_dot = route_dot.reshape(tokens_all, TOPK)
    route_gradient = (route_dot - lax.optimization_barrier(jnp.sum(route_share * route_dot, axis=-1, keepdims=True))) / route_total
    normed_cot, unused = lax.scan(expert_backward, jnp.zeros((tokens_all, D), jnp.float32), stacked_all)
    gained = norm_gain * normed_cot
    hidden_cot = inverse * gained - hidden_float * inverse ** 3 * lax.optimization_barrier(jnp.mean(hidden_float * gained, axis=-1, keepdims=True))
    residual_gradient = (cot_float + hidden_cot).astype(jnp.bfloat16)
    query_list, key_list, value_list = ([], [], [])
    for seq_index in range(SEQS):
        query_seq, key_seq, value_seq, attended, log_sum = saved[seq_index]
        grad_out = residual_gradient[seq_index * SEQ:(seq_index + 1) * SEQ].astype(jnp.float32).reshape(SEQ, KVH, group_size, DH)
        attended_float = attended.astype(jnp.float32).reshape(SEQ, KVH, group_size, DH)
        query_grad, key_grad, value_grad = attend_backward(query_seq, key_seq, value_seq, attended_float, grad_out, log_sum)
        query_list.append(query_grad)
        key_list.append(key_grad)
        value_list.append(value_grad)
    return (layer_out.reshape(SEQS, SEQ, D), residual_gradient.reshape(SEQS, SEQ, D), jnp.stack(query_list), jnp.stack(key_list), jnp.stack(value_list), route_gradient.reshape(SEQS, SEQ, TOPK))
```

```python
import jax
import jax.numpy as jnp
from jax import lax
from jax.sharding import Mesh, PartitionSpec as P

H = 16
KVH = 2
DH = 128
TOPK = 8

NEG = -1e30
EPSILON = 1e-06
F32 = jnp.float32
BF16 = jnp.bfloat16


def dot_f32(a, b, dims):
    return lax.dot_general(a, b, (dims, ((), ())), preferred_element_type=F32)


def flip_axis(value, name):
    return lax.ppermute(value, name, [(0, 1), (1, 0)])


def flip_xy(value):
    return lax.ppermute(value, ("x", "y"), [(i, 3 - i) for i in range(4)])


def ring_up(value):
    size = lax.axis_size("z")
    return lax.ppermute(value, "z", [(i, (i + 1) % size) for i in range(size)])


def to_chips(blocks):
    return [
        blocks[0],
        flip_axis(blocks[1], "y"),
        flip_axis(blocks[2], "x"),
        flip_xy(blocks[3]),
    ]


def three_parts(value):
    high = value.astype(BF16)
    rest = value - high.astype(F32)
    middle = rest.astype(BF16)
    low = (rest - middle.astype(F32)).astype(BF16)
    return high, middle, low


def per_device(
    residual,
    query_heads,
    key_heads,
    value_heads,
    norm_gain,
    chosen_experts,
    route_weights,
    gate_weight,
    up_weight,
    down_weight,
    cotangent,
):
    rows = residual.shape[1]
    width = residual.shape[2]
    kv_width = key_heads.shape[2]
    group = H // KVH
    planes = lax.axis_size("z")
    experts = planes * 8
    scale = DH ** (-0.5)
    capacity = (9 * rows * TOPK + 8 * experts - 1) // (8 * experts)
    capacity = (capacity + 3) // 4 * 4
    chip_rows = 2 * capacity
    z_index = lax.axis_index("z")
    x_index = lax.axis_index("x")
    y_index = lax.axis_index("y")
    core_index = lax.axis_index("core")

    chosen = chosen_experts[0]
    share_raw = route_weights[0]
    route_total = jnp.sum(share_raw, axis=-1, keepdims=True)
    route_share = share_raw / route_total
    hits = chosen[:, :, None] == jnp.arange(experts, dtype=jnp.int32)
    hit = jnp.any(hits, axis=1)
    share_table = jnp.sum(jnp.where(hits, route_share[:, :, None], 0.0), axis=1)
    below = (jnp.arange(rows)[:, None] > jnp.arange(rows)[None, :]).astype(BF16)
    earlier = dot_f32(below, hit.astype(BF16), ((1,), (0,)))
    slot_table = jnp.where(hit, earlier, -1.0)
    cot_own = cotangent[0]
    cot_float = cot_own.astype(F32)
    payload = jnp.concatenate(
        [cot_own, slot_table.astype(BF16)] + list(three_parts(share_table)), axis=1
    )

    kv_own = jnp.concatenate([key_heads[0], value_heads[0]], axis=1)
    ctx_count = planes * 2
    kv_blocks = [kv_own]
    for step in range(1, ctx_count):
        kv_blocks.append(
            lax.ppermute(
                kv_own, ("z", "x"), [(i, (i + step) % ctx_count) for i in range(ctx_count)]
            )
        )
    kv_all = jnp.concatenate(kv_blocks, axis=0)
    ctx_index = z_index * 2 + x_index
    key_all = kv_all[:, :kv_width].reshape(-1, KVH, DH)
    value_all = kv_all[:, kv_width:].reshape(-1, KVH, DH)
    key_block_place = jnp.mod(ctx_index - jnp.arange(ctx_count, dtype=jnp.int32), ctx_count)
    key_place = (key_block_place[:, None] * rows + jnp.arange(rows, dtype=jnp.int32)).reshape(-1)
    query_place = ctx_index * rows + jnp.arange(rows, dtype=jnp.int32)
    allowed = key_place[None, :] <= query_place[:, None]

    def own_columns(table):
        plane = lax.dynamic_slice_in_dim(table, z_index * 8, 8, axis=1)
        columns = []
        for chip in range(4):
            at = ((x_index ^ (chip >> 1)) * 2 + (y_index ^ (chip & 1))) * 2 + core_index
            columns.append(lax.dynamic_slice_in_dim(plane, at, 1, axis=1)[:, 0])
        return jnp.stack(columns)

    slot_ids = jnp.arange(capacity, dtype=F32)
    pick_steps = []
    share_steps = []
    cot_steps = []
    block = payload
    for step in range(planes):
        if step:
            block = ring_up(block)
        both = [block, flip_axis(block, "core")]
        picks = []
        shares = []
        for which, part in enumerate(both):
            slots = own_columns(part[:, width : width + experts].astype(F32))
            share = own_columns(
                part[:, width + experts : width + 2 * experts].astype(F32)
                + part[:, width + 2 * experts : width + 3 * experts].astype(F32)
                + part[:, width + 3 * experts :].astype(F32)
            )
            pick = slots[:, None, :] == slot_ids[None, :, None]
            empty = jnp.zeros_like(pick)
            picks.append(
                jnp.concatenate([pick, empty] if which == 0 else [empty, pick], axis=2)
            )
            shares.append(jnp.sum(jnp.where(pick, share[:, None, :], 0.0), axis=2))
        pick = jnp.stack(picks, axis=1).reshape(4 * chip_rows, 2 * rows).astype(BF16)
        share_rows = jnp.stack(shares, axis=1).reshape(4 * chip_rows, 1)
        pick_steps.append(pick)
        share_steps.append(share_rows)
        tokens = jnp.concatenate([part[:, :width] for part in both], axis=0)
        sent = (dot_f32(pick, tokens, ((1,), (0,))) * share_rows).astype(BF16)
        arrived = to_chips([sent[q * chip_rows : (q + 1) * chip_rows] for q in range(4)])
        cot_steps.append(jnp.concatenate(arrived, axis=0))

    query = query_heads[0].reshape(rows, KVH, group, DH)
    scores = (
        jnp.einsum("ikgd,jkd->kgij", query, key_all, preferred_element_type=F32) * scale
    )
    scores = jnp.where(allowed, scores, NEG)
    row_max = jnp.max(scores, axis=-1, keepdims=True)
    weights = jnp.exp(scores - row_max)
    row_sum = jnp.sum(weights, axis=-1, keepdims=True)
    attended = (
        jnp.einsum("kgij,jkd->kgid", weights.astype(BF16), value_all, preferred_element_type=F32)
        / row_sum
    )
    log_sum = row_max + jnp.log(row_sum)
    attended = jnp.transpose(attended, (2, 0, 1, 3)).reshape(rows, width).astype(BF16)
    hidden = (residual[0].astype(F32) + attended.astype(F32)).astype(BF16)
    hidden_float = hidden.astype(F32)
    inverse = lax.rsqrt(jnp.mean(hidden_float * hidden_float, axis=-1, keepdims=True) + EPSILON)
    normed = (hidden_float * inverse * norm_gain).astype(BF16)

    normed_steps = []
    block = normed
    for step in range(planes):
        if step:
            block = ring_up(block)
        tokens = jnp.concatenate([block, flip_axis(block, "core")], axis=0)
        sent = dot_f32(pick_steps[step], tokens, ((1,), (0,))).astype(BF16)
        arrived = to_chips([sent[q * chip_rows : (q + 1) * chip_rows] for q in range(4)])
        normed_steps.append(jnp.concatenate(arrived, axis=0))

    gate_mat = gate_weight[0]
    up_mat = up_weight[0]
    down_mat = down_weight[0]
    order = list(range(1, planes)) + [0]
    produced_steps = {}
    row_cot_steps = {}
    dot_steps = [None] * planes
    for step in order:
        incoming = normed_steps[step]
        cot_in = cot_steps[step]
        gate_act = dot_f32(incoming, gate_mat, ((1,), (0,)))
        up_act = dot_f32(incoming, up_mat, ((1,), (0,)))
        act_cot = dot_f32(cot_in, down_mat, ((1,), (1,)))
        sigma = jax.nn.sigmoid(gate_act)
        gate_cot = (act_cot * up_act * sigma * (1.0 + gate_act * (1.0 - sigma))).astype(BF16)
        up_cot = (act_cot * gate_act * sigma).astype(BF16)
        row_cot_steps[step] = (
            dot_f32(gate_cot, gate_mat, ((1,), (1,))) + dot_f32(up_cot, up_mat, ((1,), (1,)))
        ).astype(BF16)
        activation = (gate_act * sigma * up_act).astype(BF16)
        produced = dot_f32(activation, down_mat, ((1,), (0,))).astype(BF16)
        produced_steps[step] = produced
        dot_steps[step] = jnp.sum(produced.astype(F32) * cot_in.astype(F32), axis=1)

    def bring_back(result_steps, weighted):
        total = None
        for step in order:
            result = result_steps[step]
            arrived = to_chips([result[q * chip_rows : (q + 1) * chip_rows] for q in range(4)])
            back = jnp.concatenate(arrived, axis=0)
            pick = pick_steps[step]
            if weighted:
                exact = pick.astype(F32) * share_steps[step]
                high = exact.astype(BF16)
                low = (exact - high.astype(F32)).astype(BF16)
                both = dot_f32(high, back, ((0,), (0,))) + dot_f32(low, back, ((0,), (0,)))
            else:
                both = dot_f32(pick, back, ((0,), (0,)))
            part = both[:rows] + flip_axis(both[rows:].astype(BF16), "core").astype(F32)
            if total is None:
                total = part
            else:
                total = ring_up(total.astype(BF16)).astype(F32) + part
        return total

    normed_cot = bring_back(row_cot_steps, False)
    gained = norm_gain * normed_cot
    hidden_cot = inverse * gained - hidden_float * inverse**3 * jnp.mean(
        hidden_float * gained, axis=-1, keepdims=True
    )
    residual_gradient = (cot_float + hidden_cot).astype(BF16)

    grad = residual_gradient.reshape(rows, KVH, group, DH)
    row_dot = jnp.einsum(
        "ikgd,ikgd->kgi", grad, attended.reshape(rows, KVH, group, DH), preferred_element_type=F32
    )
    scores = (
        jnp.einsum("ikgd,jkd->kgij", query, key_all, preferred_element_type=F32) * scale
    )
    weights = jnp.where(allowed, jnp.exp(scores - log_sum), 0.0)
    value_part = jnp.einsum(
        "kgij,ikgd->jkd", weights.astype(BF16), grad, preferred_element_type=F32
    )
    grad_weights = jnp.einsum("ikgd,jkd->kgij", grad, value_all, preferred_element_type=F32)
    grad_scores = (weights * (grad_weights - row_dot[..., None])).astype(BF16)
    query_gradient = (
        jnp.einsum("kgij,jkd->ikgd", grad_scores, key_all, preferred_element_type=F32) * scale
    )
    query_gradient = query_gradient.reshape(rows, width).astype(BF16)
    key_part = (
        jnp.einsum("kgij,ikgd->jkd", grad_scores, query, preferred_element_type=F32) * scale
    )
    kv_part = jnp.concatenate(
        [key_part.reshape(-1, kv_width), value_part.reshape(-1, kv_width)], axis=1
    )
    kv_total = kv_part[:rows]
    kv_low = kv_part.astype(BF16)
    for step in range(1, ctx_count):
        kv_total = kv_total + lax.ppermute(
            kv_low[step * rows : (step + 1) * rows],
            ("z", "x"),
            [(i, (i - step) % ctx_count) for i in range(ctx_count)],
        ).astype(F32)
    kv_total = kv_total.astype(BF16)
    key_gradient = kv_total[:, :kv_width]
    value_gradient = kv_total[:, kv_width:]

    moe_sum = bring_back(produced_steps, True)
    layer_out = (hidden_float + moe_sum).astype(BF16)

    products = jnp.stack(dot_steps).reshape(planes, 2, 2, 2, capacity)
    products = products[jnp.mod(z_index - jnp.arange(planes, dtype=jnp.int32), planes)]
    for axis, index in ((1, x_index), (2, y_index), (3, core_index)):
        products = jnp.where(index == 1, jnp.flip(products, axis), products)
    products = lax.all_to_all(
        products.reshape(experts, capacity), ("z", "x", "y", "core"), 0, 0, tiled=True
    )
    weighted_dot = jnp.sum(
        jnp.where(
            slot_table[:, :, None] == slot_ids[None, None, :], products[None], 0.0
        ),
        axis=2,
    )
    route_dot = jnp.sum(jnp.where(hits, weighted_dot[:, None, :], 0.0), axis=2) / route_share
    route_gradient = (
        route_dot - jnp.sum(route_share * route_dot, axis=-1, keepdims=True)
    ) / route_total
    return (
        layer_out[None],
        residual_gradient[None],
        query_gradient[None],
        key_gradient[None],
        value_gradient[None],
        route_gradient[None],
    )


def solution(mesh):
    fine = Mesh(
        mesh.devices.reshape(mesh.shape["ctx"] // 2, 2, mesh.shape["exp"] // 2, 2),
        ("z", "x", "y", "core"),
    )
    tokens = P(("y", "core"), ("z", "x"), None)
    expert = P(("z", "x", "y", "core"), None, None)
    return jax.shard_map(
        per_device,
        mesh=fine,
        in_specs=(tokens,) * 4 + (P(),) + (tokens,) * 2 + (expert,) * 3 + (tokens,),
        out_specs=(tokens,) * 6,
        check_vma=False,
    )
```

```python
import functools

import jax
import jax.numpy as jnp
from jax import lax
from jax.experimental import pallas as pl
from jax.experimental.pallas import tpu as pltpu
from jax.sharding import Mesh, PartitionSpec as P

H = 16
KVH = 2
DH = 128
TOPK = 8
GROUP = H // KVH
STEPS = 2

NEG = -1e30
OPT = {
    "att": lambda cot, blocks: cot[0][1:] + [blocks[-1][1], blocks[-2][1]],
    "hop": lambda step, flipped, kv, cot: {1: [flipped], 3: cot[0][1:3] + [kv[2]] if cot else []}.get(step, []),
    "flip": lambda step, kv: {1: [kv[1]], 3: kv[3:4]}.get(step, []),
    "ga": lambda kv: [],
    "nh": lambda cot, normed, step: {2: cot[1:3], 3: cot[3:] + normed[0][:1] if normed else []}.get(step, []),
    "nf": lambda normed, step: normed[0][1:3] if step == 2 else [],
    "nb": lambda normed: normed[:4],
    "hb": lambda arrivals: [arrivals[0]],
    "ea": lambda normed: [],
    "eb": lambda rows: [],
    "row1": lambda backs: [],
    "ca": lambda backs: [],
    "attb": lambda back: [],
    "hop2": lambda back: [],
}
EPSILON = 1e-06
SCALE = DH ** (-0.5)
F32 = jnp.float32
BF16 = jnp.bfloat16
I32 = jnp.int32
SMEM = pl.BlockSpec(memory_space=pltpu.SMEM)
VMEM = pl.BlockSpec(memory_space=pltpu.VMEM)
MIB = 1 << 20


def dot_f32(a, b, dims=((1,), (0,))):
    return lax.dot_general(a, b, (dims, ((), ())), preferred_element_type=F32)


def flip_axis(value, name):
    return lax.ppermute(value, name, [(0, 1), (1, 0)])


def flip_xy(value):
    return lax.ppermute(value, ("x", "y"), [(i, 3 - i) for i in range(4)])


def ring_up(value):
    size = lax.axis_size("z")
    return lax.ppermute(value, "z", [(i, (i + 1) % size) for i in range(size)])


def line_up(value):
    size = lax.axis_size("z")
    return lax.ppermute(value, "z", [(i, i + 1) for i in range(size - 1)])


def line_down(value):
    size = lax.axis_size("z")
    return lax.ppermute(value, "z", [(i + 1, i) for i in range(size - 1)])


def ring_down(value):
    size = lax.axis_size("z")
    return lax.ppermute(value, "z", [(i, (i - 1) % size) for i in range(size)])


def to_chips(blocks):
    with jax.named_scope("to_y"):
        to_y = flip_axis(blocks[1], "y")
    with jax.named_scope("to_x"):
        to_x = flip_axis(blocks[2], "x")
    with jax.named_scope("to_xy"):
        to_xy = flip_xy(blocks[3])
    return [blocks[0], to_y, to_x, to_xy]


def params(mib):
    return pltpu.CompilerParams(vmem_limit_bytes=mib * MIB)


def cost(microseconds):
    return pl.CostEstimate(flops=0, bytes_accessed=int(microseconds * 1e6), transcendentals=0)


def gated(values, *others):
    return lax.optimization_barrier((*values, *others))[: len(values)]


def after(value, *others):
    return lax.optimization_barrier((value,) + others)[0]


def routing_kernel(experts, chosen_ref, raw_ref, cot_ref, payload_ref):
    rows, width = cot_ref.shape
    chosen = chosen_ref[...]
    raw = raw_ref[...]
    share = raw / jnp.sum(raw, axis=0, keepdims=True)
    names = lax.broadcasted_iota(I32, (experts, rows), 0)
    hit = jnp.zeros((experts, rows), F32)
    table = jnp.zeros((experts, rows), F32)
    for k in range(TOPK):
        here = names == chosen[k : k + 1]
        hit = hit + jnp.where(here, 1.0, 0.0)
        table = table + jnp.where(here, share[k : k + 1], 0.0)
    before = lax.broadcasted_iota(I32, (rows, rows), 0) < lax.broadcasted_iota(I32, (rows, rows), 1)
    earlier = dot_f32(hit.astype(BF16), jnp.where(before, 1.0, 0.0).astype(BF16))
    slots = jnp.where(hit > 0.5, earlier, -1.0)
    high = table.astype(BF16).astype(F32)
    middle = (table - high).astype(BF16).astype(F32)
    low = table - high - middle
    meta = jnp.concatenate([slots, high, middle, low], axis=0).astype(BF16)
    payload_ref[:, :width] = cot_ref[...]
    for block in range(4 * experts // rows):
        payload_ref[:, width + block * rows : width + (block + 1) * rows] = meta[
            block * rows : (block + 1) * rows
        ]


def routing(chosen, raw, cotangent, experts):
    rows, width = cotangent.shape
    return pl.pallas_call(
        functools.partial(routing_kernel, experts),
        in_specs=[VMEM] * 3,
        out_specs=VMEM,
        out_shape=jax.ShapeDtypeStruct((rows, width + 4 * experts), BF16),
        compiler_params=params(16),
        cost_estimate=cost(3),
        name="routing",
    )(chosen.T, raw.T, cotangent)


def table_row(meta, kind, experts, expert):
    rows = meta.shape[0]
    block, offset = divmod(kind * experts, rows)
    part = meta[:, block * rows : (block + 1) * rows].astype(F32)[offset : offset + experts]
    here = lax.broadcasted_iota(I32, part.shape, 0) == expert
    return jnp.sum(jnp.where(here, part, 0.0), axis=0, keepdims=True)


def table_column(meta_turned, kind, experts, expert):
    rows = meta_turned[0].shape[0]
    block, offset = divmod(kind * experts, rows)
    part = meta_turned[block]
    here = lax.broadcasted_iota(I32, part.shape, 1) == expert + offset
    return jnp.sum(jnp.where(here, part, 0.0), axis=1, keepdims=True)


def gather_kernel(experts, capacity, weighted, blocks, names_ref, *refs):
    token_refs = refs[:blocks]
    meta_refs = refs[blocks : 2 * blocks]
    out_refs = refs[2 * blocks : 2 * blocks + 4]
    pick_all, share_all = refs[2 * blocks + 4 :]
    sent_rows = out_refs[0].shape[0]
    rows = token_refs[0].shape[0]

    @pl.when(pl.program_id(0) == 0)
    def _():
        metas = [ref[...] for ref in meta_refs]
        places = lax.broadcasted_iota(I32, (sent_rows, rows), 0)
        for chip in range(4):
            expert = names_ref[chip]
            share = jnp.zeros((sent_rows, rows), F32)
            for which, meta in enumerate(metas):
                slot = table_row(meta, 0, experts, expert)
                target = jnp.where(slot >= 0, slot + which * capacity, -1.0).astype(I32)
                pick = places == target
                if weighted:
                    row = (
                        table_row(meta, 1, experts, expert)
                        + table_row(meta, 2, experts, expert)
                        + table_row(meta, 3, experts, expert)
                    )
                    share = share + jnp.where(pick, row, 0.0)
                pick_all[chip, :, which * rows : (which + 1) * rows] = jnp.where(
                    pick, 1.0, 0.0
                ).astype(BF16)
            if weighted:
                share_all[chip] = jnp.sum(share, axis=1, keepdims=True)

    tokens = jnp.concatenate([ref[...] for ref in token_refs], axis=0)
    for chip in range(4):
        found = dot_f32(pick_all[chip], tokens)
        if weighted:
            found = found * share_all[chip]
        out_refs[chip][...] = found.astype(BF16)


def gather_rows(names, token_blocks, meta_blocks, width, experts, capacity, weighted):
    rows = token_blocks[0].shape[0]
    blocks = len(token_blocks)
    sent_rows = blocks * capacity
    meta_width = 4 * experts
    cut = 512
    return pl.pallas_call(
        functools.partial(gather_kernel, experts, capacity, weighted, blocks),
        grid=(width // cut,),
        in_specs=[SMEM]
        + [pl.BlockSpec((rows, cut), lambda c: (0, c))] * blocks
        + [pl.BlockSpec((rows, meta_width), lambda c: (0, width // meta_width))] * blocks,
        out_specs=[pl.BlockSpec((sent_rows, cut), lambda c: (0, c))] * 4,
        out_shape=[jax.ShapeDtypeStruct((sent_rows, width), BF16)] * 4,
        scratch_shapes=[
            pltpu.VMEM((4, sent_rows, blocks * rows), BF16),
            pltpu.VMEM((4, sent_rows, 1), F32),
        ],
        compiler_params=params(32),
        cost_estimate=cost(4),
        name="gather_weighted" if weighted else "gather_plain",
    )(names, *token_blocks, *meta_blocks)


def expert_kernel(*refs):
    normed_refs = refs[0:4]
    cot_refs = refs[4:8]
    weight_refs = refs[8:11]
    row_refs = refs[11:15]
    made_refs = refs[15:19]
    gate, up, down, normed_all, cot_all, row_all, made_all, in_sem, weight_sem, out_sem = refs[19:]
    piece = normed_refs[0].shape[0]
    half = 2 * piece

    def place(chip):
        return pl.ds(chip * piece, piece)

    normed_in = [
        pltpu.make_async_copy(normed_refs[c], normed_all.at[place(c)], in_sem.at[0, c])
        for c in range(4)
    ]
    cot_in = [
        pltpu.make_async_copy(cot_refs[c], cot_all.at[place(c)], in_sem.at[1, c]) for c in range(4)
    ]
    weight_in = [
        pltpu.make_async_copy(weight_refs[w], held, weight_sem.at[w])
        for w, held in enumerate((gate, up, down))
    ]
    for copy in normed_in[:2] + weight_in[:2] + cot_in[:2] + weight_in[2:]:
        copy.start()
    for copy in normed_in[2:] + cot_in[2:]:
        copy.start()
    copies_out = []
    for part in range(2):
        chips = (2 * part, 2 * part + 1)
        rows = pl.ds(part * half, half)
        for c in chips:
            normed_in[c].wait()
        if part == 0:
            weight_in[0].wait()
        gate_act = dot_f32(normed_all[rows], gate[...])
        if part == 0:
            weight_in[1].wait()
        up_act = dot_f32(normed_all[rows], up[...])
        for c in chips:
            cot_in[c].wait()
        if part == 0:
            weight_in[2].wait()
        act_cot = dot_f32(cot_all[rows], down[...], ((1,), (1,)))
        sigma = jax.nn.sigmoid(gate_act)
        silu = gate_act * sigma
        gate_cot = (act_cot * up_act * sigma * (1.0 + gate_act * (1.0 - sigma))).astype(BF16)
        up_cot = (act_cot * silu).astype(BF16)
        activation = (silu * up_act).astype(BF16)
        row_all[rows] = (
            dot_f32(gate_cot, gate[...], ((1,), (1,))) + dot_f32(up_cot, up[...], ((1,), (1,)))
        ).astype(BF16)
        for c in chips:
            copy = pltpu.make_async_copy(row_all.at[place(c)], row_refs[c], out_sem.at[0, c])
            copy.start()
            copies_out.append(copy)
        made_all[rows] = dot_f32(activation, down[...]).astype(BF16)
        for c in chips:
            copy = pltpu.make_async_copy(made_all.at[place(c)], made_refs[c], out_sem.at[1, c])
            copy.start()
            copies_out.append(copy)
    for copy in copies_out:
        copy.wait()


def run_expert(normed_pieces, cot_pieces, gate_mat, up_mat, down_mat):
    piece, width = normed_pieces[0].shape
    anywhere = pl.BlockSpec(memory_space=pl.ANY)
    everything = pltpu.VMEM((4 * piece, width), BF16)
    result = pl.pallas_call(
        expert_kernel,
        in_specs=[anywhere] * 11,
        out_specs=[anywhere] * 8,
        out_shape=[jax.ShapeDtypeStruct((piece, width), BF16)] * 8,
        scratch_shapes=[
            pltpu.VMEM(gate_mat.shape, BF16),
            pltpu.VMEM(up_mat.shape, BF16),
            pltpu.VMEM(down_mat.shape, BF16),
        ]
        + [everything] * 4
        + [
            pltpu.SemaphoreType.DMA((2, 4)),
            pltpu.SemaphoreType.DMA((3,)),
            pltpu.SemaphoreType.DMA((2, 4)),
        ],
        compiler_params=params(60),
        cost_estimate=cost(18),
        name="expert",
    )(*normed_pieces, *cot_pieces, gate_mat, up_mat, down_mat)
    return result[0:4], result[4:8]


def combine_kernel(experts, capacity, blocks, names_ref, *refs):
    back_refs = refs[:4]
    meta_refs = refs[4 : 4 + blocks]
    own_refs = refs[4 + blocks : 4 + blocks + blocks // 2]
    other_ref = refs[4 + blocks + blocks // 2]
    pick_all = refs[5 + blocks + blocks // 2]

    @pl.when(pl.program_id(0) == 0)
    def _():
        fill_picks(
            experts, capacity, False, names_ref, back_refs[0].shape[0], meta_refs, pick_all
        )

    rows = meta_refs[0].shape[0]
    total = dot_f32(pick_all[...], jnp.concatenate([ref[...] for ref in back_refs], axis=0))
    for which in range(blocks):
        part = total[which * rows : (which + 1) * rows]
        if which % 2 == 0:
            own_refs[which // 2][...] = part
        else:
            other_ref[which // 2 * rows : (which // 2 + 1) * rows] = part.astype(BF16)


def fill_picks(experts, capacity, weighted, names_ref, piece, meta_refs, pick_all):
    rows = meta_refs[0].shape[0]
    places = lax.broadcasted_iota(I32, (rows, 4 * piece), 1)
    for which, meta_ref in enumerate(meta_refs):
        meta = meta_ref[...].astype(F32)
        turned = [meta[:, b * rows : (b + 1) * rows].T for b in range(meta.shape[1] // rows)]
        pick = jnp.zeros((rows, 4 * piece), F32)
        for chip in range(4):
            expert = names_ref[chip]
            slot = table_column(turned, 0, experts, expert)
            target = jnp.where(slot >= 0, slot + (which * capacity + chip * piece), -1.0)
            here = places == target.astype(I32)
            value = table_column(turned, 1, experts, expert) if weighted else 1.0
            pick = jnp.where(here, value, pick)
        pick_all[which * rows : (which + 1) * rows] = pick.astype(BF16)


def weighted_kernel(experts, capacity, blocks, names_ref, *refs):
    back_refs = refs[:4]
    meta_refs = refs[4 : 4 + blocks]
    cot_refs = refs[4 + blocks : 4 + 2 * blocks]
    own_refs = refs[4 + 2 * blocks : 4 + 2 * blocks + blocks // 2]
    other_ref, pick_all, dots_all = refs[4 + 2 * blocks + blocks // 2 :]
    piece, cut = back_refs[0].shape
    rows = meta_refs[0].shape[0]
    step = pl.program_id(0)

    @pl.when(step == 0)
    def _():
        fill_picks(experts, capacity, True, names_ref, piece, meta_refs, pick_all)
        dots_all[...] = jnp.zeros_like(dots_all)

    back = jnp.concatenate([ref[...] for ref in back_refs], axis=0)
    cots = jnp.concatenate([ref[...] for ref in cot_refs], axis=0)
    dots_all[...] += dot_f32(cots, back, ((1,), (1,)))
    total = dot_f32(pick_all[...], back)
    at = pl.ds(pl.multiple_of(step * cut, cut), cut)
    for which in range(blocks):
        part = total[which * rows : (which + 1) * rows]
        if which % 2 == 0:
            own_refs[which // 2][:, at] = part
        else:
            other_ref[which // 2 * rows : (which // 2 + 1) * rows, at] = part.astype(BF16)

    @pl.when(step == pl.num_programs(0) - 1)
    def _():
        width = other_ref.shape[1] - 4 * experts
        places = lax.broadcasted_iota(I32, (rows, 4 * piece), 1)
        lane = lax.broadcasted_iota(I32, (rows, 4 * experts), 1)
        for which in range(blocks):
            found = dots_all[which * rows : (which + 1) * rows]
            picked = pick_all[which * rows : (which + 1) * rows].astype(F32) > 0
            found = jnp.where(picked, found, 0.0)
            tail = jnp.zeros((rows, 4 * experts), F32)
            for chip in range(4):
                here = (places >= chip * piece) & (places < (chip + 1) * piece)
                value = jnp.sum(jnp.where(here, found, 0.0), axis=1, keepdims=True)
                for part in range(3):
                    low = value.astype(BF16).astype(F32)
                    tail = jnp.where(lane == names_ref[chip] + part * experts, low, tail)
                    value = value - low
            if which % 2 == 0:
                own_refs[which // 2][:, width:] = tail
            else:
                other_ref[which // 2 * rows : (which // 2 + 1) * rows, width:] = tail.astype(BF16)


def combine_rows(names, back, metas, width, experts, capacity, weighted):
    piece = back[0].shape[0]
    rows = metas[0].shape[0]
    blocks = len(metas)
    meta_width = 4 * experts
    cut = 512
    chunks = [pl.BlockSpec((piece, cut), lambda c: (0, c))] * 4
    metas_in = [pl.BlockSpec((rows, meta_width), lambda c: (0, width // meta_width))] * blocks
    if weighted:
        kernel = weighted_kernel
        metas_in = metas_in + [pl.BlockSpec((rows, cut), lambda c: (0, c))] * blocks
        metas = metas + metas
        width_out = width + meta_width
        own_spec = pl.BlockSpec((rows, width_out), lambda c: (0, 0))
        other_spec = pl.BlockSpec((blocks // 2 * rows, width_out), lambda c: (0, 0))
        scratch = [
            pltpu.VMEM((blocks * rows, 4 * piece), BF16),
            pltpu.VMEM((blocks * rows, 4 * piece), F32),
        ]
    else:
        kernel = combine_kernel
        width_out = width
        own_spec = pl.BlockSpec((rows, cut), lambda c: (0, c))
        other_spec = pl.BlockSpec((blocks // 2 * rows, cut), lambda c: (0, c))
        scratch = [pltpu.VMEM((blocks * rows, 4 * piece), BF16)]
    result = pl.pallas_call(
        functools.partial(kernel, experts, capacity, blocks),
        grid=(width // cut,),
        in_specs=[SMEM] + chunks + metas_in,
        out_specs=[own_spec] * (blocks // 2) + [other_spec],
        out_shape=[jax.ShapeDtypeStruct((rows, width_out), F32)] * (blocks // 2)
        + [jax.ShapeDtypeStruct((blocks // 2 * rows, width_out), BF16)],
        scratch_shapes=scratch,
        compiler_params=params(32),
        cost_estimate=cost(8),
        name="combine_weighted" if weighted else "combine_plain",
    )(names, *back, *metas)
    return result[:-1], result[-1]


def threshold(step, z_index, x_index):
    lower = jnp.where(step == 1, x_index == 1, step // 2 <= z_index)
    return jnp.where(step == 0, 0, jnp.where(lower, DH * 1024, -DH * 1024))


def stacked_heads(ref, kv_head):
    first = kv_head * GROUP
    return jnp.concatenate(
        [ref[:, (first + h) * DH : (first + h + 1) * DH] for h in range(GROUP)], axis=0
    )


def forward_kernel(count, ctx_ref, query_ref, residual_ref, gain_ref, *refs):
    kv_refs = refs[:count]
    attended_ref, hidden_ref, normed_ref, inverse_ref, log_ref = refs[count : count + 5]
    kv_all, score_all = refs[count + 5 :]
    rows = query_ref.shape[0]
    kv_width = KVH * DH
    for step in range(count):
        kv_all[2 * step * rows : (2 * step + 2) * rows] = kv_refs[step][...]
    z_index = ctx_ref[0]
    x_index = ctx_ref[1]
    shape = (rows, GROUP * rows)
    ahead = lax.broadcasted_iota(I32, shape, 0) - lax.rem(lax.broadcasted_iota(I32, shape, 1), rows)
    for kv_head in range(KVH):
        query = stacked_heads(query_ref, kv_head)

        def score(step, top):
            at = pl.ds(pl.multiple_of(step * rows, rows), rows)
            key = kv_all[at, kv_head * DH : (kv_head + 1) * DH]
            found = dot_f32(key, query, ((1,), (1,))) * SCALE
            found = jnp.where(ahead <= threshold(step, z_index, x_index), found, NEG)
            score_all[at] = found
            return jnp.maximum(top, jnp.max(found, axis=0, keepdims=True))

        top = lax.fori_loop(0, 2 * count, score, jnp.full((1, GROUP * rows), NEG, F32))

        def gather_values(step, state):
            total, mixed = state
            at = pl.ds(pl.multiple_of(step * rows, rows), rows)
            weight = jnp.exp(score_all[at] - top)
            value = kv_all[at, kv_width + kv_head * DH : kv_width + (kv_head + 1) * DH]
            total = total + jnp.sum(weight, axis=0, keepdims=True)
            mixed = mixed + dot_f32(value.T, weight.astype(BF16))
            return total, mixed

        total, mixed = lax.fori_loop(
            0,
            2 * count,
            gather_values,
            (jnp.zeros((1, GROUP * rows), F32), jnp.zeros((DH, GROUP * rows), F32)),
        )
        mixed = mixed / total
        log_sum = top + jnp.log(total)
        for h in range(GROUP):
            head = kv_head * GROUP + h
            at = slice(h * rows, (h + 1) * rows)
            attended_ref[:, head * DH : (head + 1) * DH] = mixed[:, at].T.astype(BF16)
            log_ref[head : head + 1, :] = log_sum[:, at]
    hidden = (residual_ref[...].astype(F32) + attended_ref[...].astype(F32)).astype(BF16)
    hidden_ref[...] = hidden
    wide = hidden.astype(F32)
    inverse = lax.rsqrt(jnp.mean(wide * wide, axis=1, keepdims=True) + EPSILON)
    inverse_ref[...] = inverse
    normed_ref[...] = (wide * inverse * gain_ref[...]).astype(BF16)


def attend_forward(ctx, query, residual, gain, kv_blocks):
    rows, width = query.shape
    count = len(kv_blocks)
    flat = jax.ShapeDtypeStruct((rows, width), BF16)
    return pl.pallas_call(
        functools.partial(forward_kernel, count),
        in_specs=[SMEM] + [VMEM] * (3 + count),
        out_specs=[VMEM] * 5,
        out_shape=[
            flat,
            flat,
            flat,
            jax.ShapeDtypeStruct((rows, 1), F32),
            jax.ShapeDtypeStruct((H, rows), F32),
        ],
        scratch_shapes=[
            pltpu.VMEM((2 * count * rows, 2 * KVH * DH), BF16),
            pltpu.VMEM((2 * count * rows, GROUP * rows), F32),
        ],
        compiler_params=params(60),
        cost_estimate=cost(12),
        name="attend_forward",
    )(ctx, query, residual, gain, *kv_blocks)


def backward_kernel(count, ctx_ref, *refs):
    (query_ref, attended_ref, hidden_ref, cot_ref, gain_ref, inverse_ref, log_ref) = refs[:7]
    ring_ref, own_ref, other_ref = refs[7:10]
    kv_refs = refs[10 : 10 + count]
    residual_ref, query_out = refs[10 + count : 12 + count]
    kv_outs = refs[12 + count : 12 + 2 * count]
    kv_all, part_all = refs[12 + 2 * count :]
    rows = query_ref.shape[0]
    kv_width = KVH * DH
    for step in range(count):
        kv_all[2 * step * rows : (2 * step + 2) * rows] = kv_refs[step][...]
    z_index = ctx_ref[0]
    x_index = ctx_ref[1]

    normed_cot = ring_ref[...].astype(F32) + own_ref[...] + other_ref[:rows].astype(F32)
    gained = gain_ref[...] * normed_cot
    hidden = hidden_ref[...].astype(F32)
    inverse = inverse_ref[...]
    mean = jnp.mean(hidden * gained, axis=1, keepdims=True)
    hidden_cot = inverse * gained - hidden * (inverse * inverse * inverse) * mean
    residual_ref[...] = (cot_ref[...].astype(F32) + hidden_cot).astype(BF16)

    lane = lax.broadcasted_iota(I32, (rows, DH), 1)
    dots = jnp.zeros((rows, DH), F32)
    for head in range(H):
        at = slice(head * DH, (head + 1) * DH)
        product = residual_ref[:, at].astype(F32) * attended_ref[:, at].astype(F32)
        dots = jnp.where(lane == head, jnp.sum(product, axis=1, keepdims=True), dots)
    dots = dots.T

    shape = (rows, GROUP * rows)
    ahead = lax.broadcasted_iota(I32, shape, 0) - lax.rem(lax.broadcasted_iota(I32, shape, 1), rows)
    for kv_head in range(KVH):
        query = stacked_heads(query_ref, kv_head)
        grad = stacked_heads(residual_ref, kv_head)
        heads = range(kv_head * GROUP, (kv_head + 1) * GROUP)
        log_row = jnp.concatenate([log_ref[h : h + 1, :] for h in heads], axis=1)
        dot_row = jnp.concatenate([dots[h : h + 1, :] for h in heads], axis=1)
        key_at = slice(kv_head * DH, (kv_head + 1) * DH)
        value_at = slice(kv_width + kv_head * DH, kv_width + (kv_head + 1) * DH)

        def visit(step, query_grad):
            at = pl.ds(pl.multiple_of(step * rows, rows), rows)
            key = kv_all[at, key_at]
            value = kv_all[at, value_at]
            found = dot_f32(key, query, ((1,), (1,))) * SCALE
            weight = jnp.where(ahead <= threshold(step, z_index, x_index), jnp.exp(found - log_row), 0.0)
            grad_weight = dot_f32(value, grad, ((1,), (1,)))
            score_cot = (weight * (grad_weight - dot_row)).astype(BF16)
            part_all[at, value_at] = dot_f32(weight.astype(BF16), grad)
            part_all[at, key_at] = dot_f32(score_cot, query) * SCALE
            return query_grad + dot_f32(key.T, score_cot)

        query_grad = lax.fori_loop(0, 2 * count, visit, jnp.zeros((DH, GROUP * rows), F32))
        query_grad = query_grad * SCALE
        for h in range(GROUP):
            head = kv_head * GROUP + h
            query_out[:, head * DH : (head + 1) * DH] = query_grad[
                :, h * rows : (h + 1) * rows
            ].T.astype(BF16)
    for step in range(count):
        found = part_all[2 * step * rows : 2 * (step + 1) * rows]
        kv_outs[step][...] = found.astype(kv_outs[step].dtype)


def attend_backward(ctx, query, attended, hidden, cot, gain, inverse, log_sum, parts, kv_blocks):
    rows, width = query.shape
    count = len(kv_blocks)
    flat = jax.ShapeDtypeStruct((rows, width), BF16)
    kv_shape = (2 * rows, 2 * KVH * DH)
    result = pl.pallas_call(
        functools.partial(backward_kernel, count),
        in_specs=[SMEM] + [VMEM] * (10 + count),
        out_specs=[VMEM] * (2 + count),
        out_shape=[flat, flat]
        + [jax.ShapeDtypeStruct(kv_shape, F32)] * (count - 1)
        + [jax.ShapeDtypeStruct(kv_shape, BF16)],
        scratch_shapes=[
            pltpu.VMEM((2 * count * rows, 2 * KVH * DH), BF16),
            pltpu.VMEM((2 * count * rows, 2 * KVH * DH), F32),
        ],
        compiler_params=params(60),
        cost_estimate=cost(15),
        name="attend_backward",
    )(ctx, query, attended, hidden, cot, gain, inverse, log_sum, *parts, *kv_blocks)
    return result[0], result[1], result[2:]


def per_device(
    residual,
    query_heads,
    key_heads,
    value_heads,
    norm_gain,
    chosen_experts,
    route_weights,
    gate_weight,
    up_weight,
    down_weight,
    cotangent,
):
    rows = residual.shape[1]
    width = residual.shape[2]
    kv_width = key_heads.shape[2]
    planes = lax.axis_size("z")
    experts = planes * 8
    capacity = (9 * rows * TOPK + 8 * experts - 1) // (8 * experts)
    capacity = (capacity + 3) // 4 * 4
    z_index = lax.axis_index("z")
    x_index = lax.axis_index("x")
    y_index = lax.axis_index("y")
    core_index = lax.axis_index("core")
    groups = [list(range(first, first + STEPS)) for first in range(0, planes, STEPS)]
    names = jnp.stack(
        [
            ((z_index * 2 + (x_index ^ (chip >> 1))) * 2 + (y_index ^ (chip & 1))) * 2 + core_index
            for chip in range(4)
        ]
    ).astype(I32)
    ctx = jnp.stack([z_index, x_index]).astype(I32)
    gain = norm_gain[None, :]

    kv_own = jnp.concatenate([key_heads[0], value_heads[0]], axis=1)
    with jax.named_scope("kv_flip"):
        kv_flipped = flip_axis(kv_own, "x")
    kv_blocks = [jnp.concatenate([kv_own, kv_flipped], axis=0)]
    with jax.named_scope("kv_hop"):
        for step in range(1, planes):
            kv_blocks.append(line_up(kv_blocks[-1]))

    chosen = chosen_experts[0]
    payload = routing(chosen, route_weights[0], cotangent[0], experts)

    def gather(blocks, index, weighted, *earlier):
        sent = gather_rows(
            after(names, *earlier), blocks, metas[index], width, experts, capacity, weighted
        )
        return to_chips(sent)

    def hop(block, *earlier):
        with jax.named_scope("hop"):
            return ring_up(after(block, *earlier))

    def both_cores(block, *earlier):
        with jax.named_scope("flip"):
            return [block, flip_axis(after(block, *earlier), "core")]

    cot_pieces = []
    metas = []
    payload_blocks = []
    block = payload
    for index, group in enumerate(groups):
        for step in group:
            with jax.named_scope("cot"):
                earlier = []
                if step:
                    waits = OPT["hop"](step, kv_flipped, kv_blocks, cot_pieces)
                    block = hop(block, *waits)
                    earlier = OPT["flip"](step, kv_blocks)
                payload_blocks.append(both_cores(block, *earlier))
        metas.append(sum([payload_blocks[step] for step in group], []))
        if index == 0:
            with jax.named_scope("cot0"):
                cot_pieces.append(gather(metas[0], 0, True, *OPT["ga"](kv_blocks)))
    attended, hidden, normed, inverse, log_sum = attend_forward(
        after(ctx, *OPT["att"](cot_pieces, payload_blocks)),
        query_heads[0],
        residual[0],
        gain,
        kv_blocks,
    )
    order = inverse
    for index in range(1, len(groups)):
        with jax.named_scope("cot1"):
            cot_pieces.append(gather(metas[index], index, True, order, *cot_pieces[-1][1:]))
        order = cot_pieces[-1][0]

    normed_blocks = []
    normed_pieces = []
    earlier = cot_pieces[-1][:3]
    block = normed
    for index, group in enumerate(groups):
        for step in group:
            with jax.named_scope("normed"):
                if step:
                    block = hop(block, *OPT["nh"](cot_pieces[-1], normed_pieces, step))
                normed_blocks.append(both_cores(block, *OPT["nf"](normed_pieces, step)))
        tokens = sum([normed_blocks[step] for step in group], [])
        with jax.named_scope("normed1" if index else "normed0"):
            normed_pieces.append(gather(tokens, index, False, *earlier))
        earlier = OPT["nb"](normed_pieces[-1]) + cot_pieces[-1][3:]
    order = normed_pieces[-1][0]
    row_pieces = []
    made_pieces = []
    for index in range(len(groups)):
        pieces = normed_pieces[index]
        waits = OPT['ea'](normed_pieces) if index == 0 else OPT['eb'](row_first)
        pieces = [after(pieces[0], order, *waits)] + pieces[1:]
        row_cot, produced = run_expert(
            pieces, cot_pieces[index], gate_weight[0], up_weight[0], down_weight[0]
        )
        order = row_cot[0]
        row_first = row_cot
        row_pieces.append(row_cot)
        made_pieces.append(produced)

    def sums(back, index, weighted, *earlier):
        own, other = combine_rows(
            after(names, *earlier), back, metas[index], width, experts, capacity, weighted
        )
        with jax.named_scope("sum_flip"):
            return own, flip_axis(other, "core")

    def term(parts, at):
        own, other = parts
        return own[at] + other[at * rows : (at + 1) * rows].astype(F32)

    row_backs = []
    row_sums = []
    for index in range(len(groups)):
        with jax.named_scope("row1" if index else "row0"):
            row_backs.append(to_chips(gated(row_pieces[index], *OPT['row1'](row_backs))))
    for index in range(len(groups)):
        with jax.named_scope("row1" if index else "row0"):
            later = [first_moved] if index else OPT['ca'](row_backs)
            row_sums.append(sums(row_backs[index], index, False, order, *later))
        if index == 0:
            total = term(row_sums[0], 1).astype(BF16)
            with jax.named_scope("row_hop"):
                first_moved = ring_up(total)
        order = row_sums[-1][0][0]

    made_backs = [None] * len(groups)
    made_sums = [None] * len(groups)
    earlier = row_backs[-1]
    for index in reversed(range(len(groups))):
        with jax.named_scope("made1" if index else "made0"):
            made_backs[index] = to_chips(gated(made_pieces[index], *earlier[1:]))
        earlier = made_backs[index]

    with jax.named_scope("row_hop"):
        for step in range(2, planes):
            if step == 2:
                moved = first_moved
            else:
                moved = ring_up(after(total, *OPT['hop2'](made_backs[-1])))
            total = moved.astype(F32) + term(row_sums[step // STEPS], step % STEPS)
            total = total.astype(BF16)
        cot_terms = (ring_up(total), row_sums[0][0][0], row_sums[0][1])
    for index in reversed(range(1, len(groups))):
        with jax.named_scope("made1"):
            made_sums[index] = sums(made_backs[index], index, True, cot_terms[0])

    residual_gradient, query_gradient, kv_parts = attend_backward(
        after(ctx, made_sums[1][0][0], *OPT['attb'](made_backs[0])),
        query_heads[0],
        attended,
        hidden,
        cotangent[0],
        gain,
        inverse,
        log_sum,
        cot_terms,
        kv_blocks,
    )
    kv_total = kv_parts[-1]
    arrivals = []
    kv_low = []
    for step in reversed(range(planes - 1)):
        with jax.named_scope("kv_back_hop"):
            arrivals.append(line_down(kv_total.astype(BF16)))
        kv_total = arrivals[-1].astype(F32) + kv_parts[step]
        if step:
            kv_total = kv_total.astype(BF16)
            kv_low.append(kv_total)
    with jax.named_scope("kv_back_flip"):
        kv_flipped_total = flip_axis(kv_total[rows:].astype(BF16), "x")
    kv_total = kv_total[:rows] + kv_flipped_total.astype(F32)
    kv_total = kv_total.astype(BF16)
    key_gradient = kv_total[:, :kv_width]
    value_gradient = kv_total[:, kv_width:]

    made_total = None
    for step in reversed(range(STEPS, planes)):
        part = term(made_sums[step // STEPS], step % STEPS)
        with jax.named_scope("made_hop"):
            if made_total is not None:
                part = after(made_total, *OPT['hb'](arrivals)).astype(F32) + part
            made_total = ring_down(part.astype(BF16))
    with jax.named_scope("made0"):
        made_sums[0] = sums(made_backs[0], 0, True, kv_low[0])
    for step in reversed(range(STEPS)):
        moe_sum = made_total.astype(F32) + term(made_sums[0], step)
        if step:
            with jax.named_scope("made_hop"):
                made_total = ring_down(moe_sum.astype(BF16))
    layer_out = (hidden.astype(F32) + moe_sum[:, :width]).astype(BF16)

    found = moe_sum[:, width:].reshape(rows, 4, experts)
    found = found[:, 0] + found[:, 1] + found[:, 2]
    hits = chosen[:, :, None] == jnp.arange(experts, dtype=I32)
    route_dot = jnp.sum(jnp.where(hits, found[:, None, :], 0.0), axis=2)
    share_raw = route_weights[0]
    route_total = jnp.sum(share_raw, axis=1, keepdims=True)
    route_share = share_raw / route_total
    route_gradient = (
        route_dot - jnp.sum(route_share * route_dot, axis=1, keepdims=True)
    ) / route_total
    return (
        layer_out[None],
        residual_gradient[None],
        query_gradient[None],
        key_gradient[None],
        value_gradient[None],
        route_gradient[None],
    )


def solution(mesh):
    fine = Mesh(
        mesh.devices.reshape(mesh.shape["ctx"] // 2, 2, mesh.shape["exp"] // 2, 2),
        ("z", "x", "y", "core"),
    )
    tokens = P(("y", "core"), ("z", "x"), None)
    expert = P(("z", "x", "y", "core"), None, None)
    return jax.shard_map(
        per_device,
        mesh=fine,
        in_specs=(tokens,) * 4 + (P(),) + (tokens,) * 2 + (expert,) * 3 + (tokens,),
        out_specs=(tokens,) * 6,
        check_vma=False,
    )
```

```python
import functools

import jax
import jax.numpy as jnp
from jax import lax
from jax.experimental import pallas as pl
from jax.experimental.pallas import tpu as pltpu
from jax.sharding import Mesh, PartitionSpec as P

H = 16
KVH = 2
DH = 128
TOPK = 8
GROUP = H // KVH
STEPS = 2

NEG = -1e30
OPT = {
    "att": lambda cot, blocks: [cot[-1][0]],
    "hop": lambda step, flipped, kv, cot: {1: [flipped], 3: cot[0][1:3] + [kv[2]] if cot else []}.get(step, []),
    "flip": lambda step, kv: {1: [kv[1]], 3: kv[3:4]}.get(step, []),
    "ga": lambda kv: [],
    "nh": lambda cot, normed, step: {2: cot[1:3], 3: cot[3:] + normed[0][:1] if normed else []}.get(step, []),
    "nf": lambda normed, step: normed[0][1:3] if step == 2 else [],
    "nb": lambda normed: normed[:4],
    "ea": lambda normed: [],
    "eb": lambda rows: [],
    "row1": lambda backs: [],
    "ca": lambda backs: [],
    "attb": lambda back: [],
    "hop2": lambda back: [],
}
EPSILON = 1e-06
SCALE = DH ** (-0.5)
F32 = jnp.float32
BF16 = jnp.bfloat16
I32 = jnp.int32
SMEM = pl.BlockSpec(memory_space=pltpu.SMEM)
VMEM = pl.BlockSpec(memory_space=pltpu.VMEM)
MIB = 1 << 20


def dot_f32(a, b, dims=((1,), (0,))):
    return lax.dot_general(a, b, (dims, ((), ())), preferred_element_type=F32)


def flip_axis(value, name):
    return lax.ppermute(value, name, [(0, 1), (1, 0)])


def flip_xy(value):
    return lax.ppermute(value, ("x", "y"), [(i, 3 - i) for i in range(4)])


def ring_up(value):
    size = lax.axis_size("z")
    return lax.ppermute(value, "z", [(i, (i + 1) % size) for i in range(size)])


def line_up(value):
    size = lax.axis_size("z")
    return lax.ppermute(value, "z", [(i, i + 1) for i in range(size - 1)])


def line_down(value):
    size = lax.axis_size("z")
    return lax.ppermute(value, "z", [(i + 1, i) for i in range(size - 1)])


def ring_down(value):
    size = lax.axis_size("z")
    return lax.ppermute(value, "z", [(i, (i - 1) % size) for i in range(size)])


def to_chips(blocks):
    with jax.named_scope("to_y"):
        to_y = flip_axis(blocks[1], "y")
    with jax.named_scope("to_x"):
        to_x = flip_axis(blocks[2], "x")
    with jax.named_scope("to_xy"):
        to_xy = flip_xy(blocks[3])
    return [blocks[0], to_y, to_x, to_xy]


def params(mib):
    return pltpu.CompilerParams(vmem_limit_bytes=mib * MIB)


def cost(microseconds):
    return pl.CostEstimate(flops=0, bytes_accessed=int(microseconds * 1e6), transcendentals=0)


def gated(values, *others):
    return lax.optimization_barrier((*values, *others))[: len(values)]


def after(value, *others):
    return lax.optimization_barrier((value,) + others)[0]


def routing_kernel(experts, chosen_ref, raw_ref, cot_ref, payload_ref):
    rows, width = cot_ref.shape
    chosen = chosen_ref[...]
    raw = raw_ref[...]
    share = raw / jnp.sum(raw, axis=0, keepdims=True)
    names = lax.broadcasted_iota(I32, (experts, rows), 0)
    hit = jnp.zeros((experts, rows), F32)
    table = jnp.zeros((experts, rows), F32)
    for k in range(TOPK):
        here = names == chosen[k : k + 1]
        hit = hit + jnp.where(here, 1.0, 0.0)
        table = table + jnp.where(here, share[k : k + 1], 0.0)
    before = lax.broadcasted_iota(I32, (rows, rows), 0) < lax.broadcasted_iota(I32, (rows, rows), 1)
    earlier = dot_f32(hit.astype(BF16), jnp.where(before, 1.0, 0.0).astype(BF16))
    slots = jnp.where(hit > 0.5, earlier, -1.0)
    high = table.astype(BF16).astype(F32)
    middle = (table - high).astype(BF16).astype(F32)
    low = table - high - middle
    meta = jnp.concatenate([slots, high, middle, low], axis=0).astype(BF16)
    payload_ref[:, :width] = cot_ref[...]
    for block in range(4 * experts // rows):
        payload_ref[:, width + block * rows : width + (block + 1) * rows] = meta[
            block * rows : (block + 1) * rows
        ]


def routing(chosen, raw, cotangent, experts):
    rows, width = cotangent.shape
    return pl.pallas_call(
        functools.partial(routing_kernel, experts),
        in_specs=[VMEM] * 3,
        out_specs=VMEM,
        out_shape=jax.ShapeDtypeStruct((rows, width + 4 * experts), BF16),
        compiler_params=params(16),
        cost_estimate=cost(3),
        name="routing",
    )(chosen.T, raw.T, cotangent)


def table_row(meta, kind, experts, expert):
    rows = meta.shape[0]
    block, offset = divmod(kind * experts, rows)
    part = meta[:, block * rows : (block + 1) * rows].astype(F32)[offset : offset + experts]
    here = lax.broadcasted_iota(I32, part.shape, 0) == expert
    return jnp.sum(jnp.where(here, part, 0.0), axis=0, keepdims=True)


def table_column(meta_turned, kind, experts, expert):
    rows = meta_turned[0].shape[0]
    block, offset = divmod(kind * experts, rows)
    part = meta_turned[block]
    here = lax.broadcasted_iota(I32, part.shape, 1) == expert + offset
    return jnp.sum(jnp.where(here, part, 0.0), axis=1, keepdims=True)


def gather_kernel(experts, capacity, weighted, blocks, names_ref, *refs):
    token_refs = refs[:blocks]
    meta_refs = refs[blocks : 2 * blocks]
    out_refs = refs[2 * blocks : 2 * blocks + 4]
    pick_all, share_all = refs[2 * blocks + 4 :]
    sent_rows = out_refs[0].shape[0]
    rows = token_refs[0].shape[0]

    @pl.when(pl.program_id(0) == 0)
    def _():
        metas = [ref[...] for ref in meta_refs]
        places = lax.broadcasted_iota(I32, (sent_rows, rows), 0)
        for chip in range(4):
            expert = names_ref[chip]
            share = jnp.zeros((sent_rows, rows), F32)
            for which, meta in enumerate(metas):
                slot = table_row(meta, 0, experts, expert)
                target = jnp.where(slot >= 0, slot + which * capacity, -1.0).astype(I32)
                pick = places == target
                if weighted:
                    row = (
                        table_row(meta, 1, experts, expert)
                        + table_row(meta, 2, experts, expert)
                        + table_row(meta, 3, experts, expert)
                    )
                    share = share + jnp.where(pick, row, 0.0)
                pick_all[chip, :, which * rows : (which + 1) * rows] = jnp.where(
                    pick, 1.0, 0.0
                ).astype(BF16)
            if weighted:
                share_all[chip] = jnp.sum(share, axis=1, keepdims=True)

    tokens = jnp.concatenate([ref[...] for ref in token_refs], axis=0)
    for chip in range(4):
        found = dot_f32(pick_all[chip], tokens)
        if weighted:
            found = found * share_all[chip]
        out_refs[chip][...] = found.astype(BF16)


def gather_rows(names, token_blocks, meta_blocks, width, experts, capacity, weighted):
    rows = token_blocks[0].shape[0]
    blocks = len(token_blocks)
    sent_rows = blocks * capacity
    meta_width = 4 * experts
    cut = 512
    return pl.pallas_call(
        functools.partial(gather_kernel, experts, capacity, weighted, blocks),
        grid=(width // cut,),
        in_specs=[SMEM]
        + [pl.BlockSpec((rows, cut), lambda c: (0, c))] * blocks
        + [pl.BlockSpec((rows, meta_width), lambda c: (0, width // meta_width))] * blocks,
        out_specs=[pl.BlockSpec((sent_rows, cut), lambda c: (0, c))] * 4,
        out_shape=[jax.ShapeDtypeStruct((sent_rows, width), BF16)] * 4,
        scratch_shapes=[
            pltpu.VMEM((4, sent_rows, blocks * rows), BF16),
            pltpu.VMEM((4, sent_rows, 1), F32),
        ],
        compiler_params=params(32),
        cost_estimate=cost(4),
        name="gather_weighted" if weighted else "gather_plain",
    )(names, *token_blocks, *meta_blocks)


def expert_kernel(*refs):
    normed_refs = refs[0:4]
    cot_refs = refs[4:8]
    weight_refs = refs[8:11]
    row_refs = refs[11:15]
    made_refs = refs[15:19]
    gate, up, down, normed_all, cot_all, row_all, made_all, in_sem, weight_sem, out_sem = refs[19:]
    piece = normed_refs[0].shape[0]
    half = 2 * piece

    def place(chip):
        return pl.ds(chip * piece, piece)

    normed_in = [
        pltpu.make_async_copy(normed_refs[c], normed_all.at[place(c)], in_sem.at[0, c])
        for c in range(4)
    ]
    cot_in = [
        pltpu.make_async_copy(cot_refs[c], cot_all.at[place(c)], in_sem.at[1, c]) for c in range(4)
    ]
    weight_in = [
        pltpu.make_async_copy(weight_refs[w], held, weight_sem.at[w])
        for w, held in enumerate((gate, up, down))
    ]
    for copy in normed_in[:2] + weight_in[:2] + cot_in[:2] + weight_in[2:]:
        copy.start()
    for copy in normed_in[2:] + cot_in[2:]:
        copy.start()
    copies_out = []
    for part in range(2):
        chips = (2 * part, 2 * part + 1)
        rows = pl.ds(part * half, half)
        for c in chips:
            normed_in[c].wait()
        if part == 0:
            weight_in[0].wait()
        gate_act = dot_f32(normed_all[rows], gate[...])
        if part == 0:
            weight_in[1].wait()
        up_act = dot_f32(normed_all[rows], up[...])
        for c in chips:
            cot_in[c].wait()
        if part == 0:
            weight_in[2].wait()
        act_cot = dot_f32(cot_all[rows], down[...], ((1,), (1,)))
        sigma = jax.nn.sigmoid(gate_act)
        silu = gate_act * sigma
        gate_cot = (act_cot * up_act * sigma * (1.0 + gate_act * (1.0 - sigma))).astype(BF16)
        up_cot = (act_cot * silu).astype(BF16)
        activation = (silu * up_act).astype(BF16)
        row_all[rows] = (
            dot_f32(gate_cot, gate[...], ((1,), (1,))) + dot_f32(up_cot, up[...], ((1,), (1,)))
        ).astype(BF16)
        for c in chips:
            copy = pltpu.make_async_copy(row_all.at[place(c)], row_refs[c], out_sem.at[0, c])
            copy.start()
            copies_out.append(copy)
        made_all[rows] = dot_f32(activation, down[...]).astype(BF16)
        for c in chips:
            copy = pltpu.make_async_copy(made_all.at[place(c)], made_refs[c], out_sem.at[1, c])
            copy.start()
            copies_out.append(copy)
    for copy in copies_out:
        copy.wait()


def run_expert(normed_pieces, cot_pieces, gate_mat, up_mat, down_mat):
    piece, width = normed_pieces[0].shape
    anywhere = pl.BlockSpec(memory_space=pl.ANY)
    everything = pltpu.VMEM((4 * piece, width), BF16)
    result = pl.pallas_call(
        expert_kernel,
        in_specs=[anywhere] * 11,
        out_specs=[anywhere] * 8,
        out_shape=[jax.ShapeDtypeStruct((piece, width), BF16)] * 8,
        scratch_shapes=[
            pltpu.VMEM(gate_mat.shape, BF16),
            pltpu.VMEM(up_mat.shape, BF16),
            pltpu.VMEM(down_mat.shape, BF16),
        ]
        + [everything] * 4
        + [
            pltpu.SemaphoreType.DMA((2, 4)),
            pltpu.SemaphoreType.DMA((3,)),
            pltpu.SemaphoreType.DMA((2, 4)),
        ],
        compiler_params=params(60),
        cost_estimate=cost(18),
        name="expert",
    )(*normed_pieces, *cot_pieces, gate_mat, up_mat, down_mat)
    return result[0:4], result[4:8]


def combine_kernel(experts, capacity, blocks, names_ref, *refs):
    back_refs = refs[:4]
    meta_refs = refs[4 : 4 + blocks]
    own_refs = refs[4 + blocks : 4 + blocks + blocks // 2]
    other_ref = refs[4 + blocks + blocks // 2]
    pick_all = refs[5 + blocks + blocks // 2]

    @pl.when(pl.program_id(0) == 0)
    def _():
        fill_picks(
            experts, capacity, False, names_ref, back_refs[0].shape[0], meta_refs, pick_all
        )

    rows = meta_refs[0].shape[0]
    total = dot_f32(pick_all[...], jnp.concatenate([ref[...] for ref in back_refs], axis=0))
    for which in range(blocks):
        part = total[which * rows : (which + 1) * rows]
        if which % 2 == 0:
            own_refs[which // 2][...] = part
        else:
            other_ref[which // 2 * rows : (which // 2 + 1) * rows] = part.astype(BF16)


def fill_picks(experts, capacity, weighted, names_ref, piece, meta_refs, pick_all):
    rows = meta_refs[0].shape[0]
    places = lax.broadcasted_iota(I32, (rows, 4 * piece), 1)
    for which, meta_ref in enumerate(meta_refs):
        meta = meta_ref[...].astype(F32)
        turned = [meta[:, b * rows : (b + 1) * rows].T for b in range(meta.shape[1] // rows)]
        pick = jnp.zeros((rows, 4 * piece), F32)
        for chip in range(4):
            expert = names_ref[chip]
            slot = table_column(turned, 0, experts, expert)
            target = jnp.where(slot >= 0, slot + (which * capacity + chip * piece), -1.0)
            here = places == target.astype(I32)
            value = table_column(turned, 1, experts, expert) if weighted else 1.0
            pick = jnp.where(here, value, pick)
        pick_all[which * rows : (which + 1) * rows] = pick.astype(BF16)


def weighted_kernel(experts, capacity, blocks, names_ref, *refs):
    back_refs = refs[:4]
    meta_refs = refs[4 : 4 + blocks]
    cot_refs = refs[4 + blocks : 4 + 2 * blocks]
    own_refs = refs[4 + 2 * blocks : 4 + 2 * blocks + blocks // 2]
    other_ref, pick_all, dots_all = refs[4 + 2 * blocks + blocks // 2 :]
    piece, cut = back_refs[0].shape
    rows = meta_refs[0].shape[0]
    step = pl.program_id(0)

    @pl.when(step == 0)
    def _():
        fill_picks(experts, capacity, True, names_ref, piece, meta_refs, pick_all)
        dots_all[...] = jnp.zeros_like(dots_all)

    back = jnp.concatenate([ref[...] for ref in back_refs], axis=0)
    cots = jnp.concatenate([ref[...] for ref in cot_refs], axis=0)
    dots_all[...] += dot_f32(cots, back, ((1,), (1,)))
    total = dot_f32(pick_all[...], back)
    at = pl.ds(pl.multiple_of(step * cut, cut), cut)
    for which in range(blocks):
        part = total[which * rows : (which + 1) * rows]
        if which % 2 == 0:
            own_refs[which // 2][:, at] = part
        else:
            other_ref[which // 2 * rows : (which // 2 + 1) * rows, at] = part.astype(BF16)

    @pl.when(step == pl.num_programs(0) - 1)
    def _():
        width = other_ref.shape[1] - 4 * experts
        places = lax.broadcasted_iota(I32, (rows, 4 * piece), 1)
        lane = lax.broadcasted_iota(I32, (rows, 4 * experts), 1)
        for which in range(blocks):
            found = dots_all[which * rows : (which + 1) * rows]
            picked = pick_all[which * rows : (which + 1) * rows].astype(F32) > 0
            found = jnp.where(picked, found, 0.0)
            tail = jnp.zeros((rows, 4 * experts), F32)
            for chip in range(4):
                here = (places >= chip * piece) & (places < (chip + 1) * piece)
                value = jnp.sum(jnp.where(here, found, 0.0), axis=1, keepdims=True)
                for part in range(3):
                    low = value.astype(BF16).astype(F32)
                    tail = jnp.where(lane == names_ref[chip] + part * experts, low, tail)
                    value = value - low
            if which % 2 == 0:
                own_refs[which // 2][:, width:] = tail
            else:
                other_ref[which // 2 * rows : (which // 2 + 1) * rows, width:] = tail.astype(BF16)


def combine_rows(names, back, metas, width, experts, capacity, weighted):
    piece = back[0].shape[0]
    rows = metas[0].shape[0]
    blocks = len(metas)
    meta_width = 4 * experts
    cut = 512
    chunks = [pl.BlockSpec((piece, cut), lambda c: (0, c))] * 4
    metas_in = [pl.BlockSpec((rows, meta_width), lambda c: (0, width // meta_width))] * blocks
    if weighted:
        kernel = weighted_kernel
        metas_in = metas_in + [pl.BlockSpec((rows, cut), lambda c: (0, c))] * blocks
        metas = metas + metas
        width_out = width + meta_width
        own_spec = pl.BlockSpec((rows, width_out), lambda c: (0, 0))
        other_spec = pl.BlockSpec((blocks // 2 * rows, width_out), lambda c: (0, 0))
        scratch = [
            pltpu.VMEM((blocks * rows, 4 * piece), BF16),
            pltpu.VMEM((blocks * rows, 4 * piece), F32),
        ]
    else:
        kernel = combine_kernel
        width_out = width
        own_spec = pl.BlockSpec((rows, cut), lambda c: (0, c))
        other_spec = pl.BlockSpec((blocks // 2 * rows, cut), lambda c: (0, c))
        scratch = [pltpu.VMEM((blocks * rows, 4 * piece), BF16)]
    result = pl.pallas_call(
        functools.partial(kernel, experts, capacity, blocks),
        grid=(width // cut,),
        in_specs=[SMEM] + chunks + metas_in,
        out_specs=[own_spec] * (blocks // 2) + [other_spec],
        out_shape=[jax.ShapeDtypeStruct((rows, width_out), F32)] * (blocks // 2)
        + [jax.ShapeDtypeStruct((blocks // 2 * rows, width_out), BF16)],
        scratch_shapes=scratch,
        compiler_params=params(32),
        cost_estimate=cost(8),
        name="combine_weighted" if weighted else "combine_plain",
    )(names, *back, *metas)
    return result[:-1], result[-1]


def threshold(step, z_index, x_index):
    lower = jnp.where(step == 1, x_index == 1, step // 2 <= z_index)
    return jnp.where(step == 0, 0, jnp.where(lower, DH * 1024, -DH * 1024))


def stacked_heads(ref, kv_head):
    first = kv_head * GROUP
    return jnp.concatenate(
        [ref[:, (first + h) * DH : (first + h + 1) * DH] for h in range(GROUP)], axis=0
    )


def forward_kernel(count, ctx_ref, query_ref, residual_ref, gain_ref, *refs):
    kv_refs = refs[:count]
    attended_ref, hidden_ref, normed_ref, inverse_ref, log_ref = refs[count : count + 5]
    kv_all, score_all = refs[count + 5 :]
    rows = query_ref.shape[0]
    kv_width = KVH * DH
    for step in range(count):
        kv_all[2 * step * rows : (2 * step + 2) * rows] = kv_refs[step][...]
    z_index = ctx_ref[0]
    x_index = ctx_ref[1]
    shape = (rows, GROUP * rows)
    ahead = lax.broadcasted_iota(I32, shape, 0) - lax.rem(lax.broadcasted_iota(I32, shape, 1), rows)
    for kv_head in range(KVH):
        query = stacked_heads(query_ref, kv_head)

        def score(step, top):
            at = pl.ds(pl.multiple_of(step * rows, rows), rows)
            key = kv_all[at, kv_head * DH : (kv_head + 1) * DH]
            found = dot_f32(key, query, ((1,), (1,))) * SCALE
            found = jnp.where(ahead <= threshold(step, z_index, x_index), found, NEG)
            score_all[at] = found
            return jnp.maximum(top, jnp.max(found, axis=0, keepdims=True))

        top = lax.fori_loop(0, 2 * count, score, jnp.full((1, GROUP * rows), NEG, F32))

        def gather_values(step, state):
            total, mixed = state
            at = pl.ds(pl.multiple_of(step * rows, rows), rows)
            weight = jnp.exp(score_all[at] - top)
            value = kv_all[at, kv_width + kv_head * DH : kv_width + (kv_head + 1) * DH]
            total = total + jnp.sum(weight, axis=0, keepdims=True)
            mixed = mixed + dot_f32(value.T, weight.astype(BF16))
            return total, mixed

        total, mixed = lax.fori_loop(
            0,
            2 * count,
            gather_values,
            (jnp.zeros((1, GROUP * rows), F32), jnp.zeros((DH, GROUP * rows), F32)),
        )
        mixed = mixed / total
        log_sum = top + jnp.log(total)
        for h in range(GROUP):
            head = kv_head * GROUP + h
            at = slice(h * rows, (h + 1) * rows)
            attended_ref[:, head * DH : (head + 1) * DH] = mixed[:, at].T.astype(BF16)
            log_ref[head : head + 1, :] = log_sum[:, at]
    hidden = (residual_ref[...].astype(F32) + attended_ref[...].astype(F32)).astype(BF16)
    hidden_ref[...] = hidden
    wide = hidden.astype(F32)
    inverse = lax.rsqrt(jnp.mean(wide * wide, axis=1, keepdims=True) + EPSILON)
    inverse_ref[...] = inverse
    normed_ref[...] = (wide * inverse * gain_ref[...]).astype(BF16)


def attend_forward(ctx, query, residual, gain, kv_blocks):
    rows, width = query.shape
    count = len(kv_blocks)
    flat = jax.ShapeDtypeStruct((rows, width), BF16)
    return pl.pallas_call(
        functools.partial(forward_kernel, count),
        in_specs=[SMEM] + [VMEM] * (3 + count),
        out_specs=[VMEM] * 5,
        out_shape=[
            flat,
            flat,
            flat,
            jax.ShapeDtypeStruct((rows, 1), F32),
            jax.ShapeDtypeStruct((H, rows), F32),
        ],
        scratch_shapes=[
            pltpu.VMEM((2 * count * rows, 2 * KVH * DH), BF16),
            pltpu.VMEM((2 * count * rows, GROUP * rows), F32),
        ],
        compiler_params=params(60),
        cost_estimate=cost(12),
        name="attend_forward",
    )(ctx, query, residual, gain, *kv_blocks)


def backward_kernel(count, ctx_ref, *refs):
    (query_ref, attended_ref, hidden_ref, cot_ref, gain_ref, inverse_ref, log_ref) = refs[:7]
    ring_ref, own_ref, other_ref = refs[7:10]
    kv_refs = refs[10 : 10 + count]
    residual_ref, query_out = refs[10 + count : 12 + count]
    kv_outs = refs[12 + count : 12 + 2 * count]
    kv_all, part_all = refs[12 + 2 * count :]
    rows = query_ref.shape[0]
    kv_width = KVH * DH
    for step in range(count):
        kv_all[2 * step * rows : (2 * step + 2) * rows] = kv_refs[step][...]
    z_index = ctx_ref[0]
    x_index = ctx_ref[1]

    normed_cot = ring_ref[...].astype(F32) + own_ref[...] + other_ref[:rows].astype(F32)
    gained = gain_ref[...] * normed_cot
    hidden = hidden_ref[...].astype(F32)
    inverse = inverse_ref[...]
    mean = jnp.mean(hidden * gained, axis=1, keepdims=True)
    hidden_cot = inverse * gained - hidden * (inverse * inverse * inverse) * mean
    residual_ref[...] = (cot_ref[...].astype(F32) + hidden_cot).astype(BF16)

    lane = lax.broadcasted_iota(I32, (rows, DH), 1)
    dots = jnp.zeros((rows, DH), F32)
    for head in range(H):
        at = slice(head * DH, (head + 1) * DH)
        product = residual_ref[:, at].astype(F32) * attended_ref[:, at].astype(F32)
        dots = jnp.where(lane == head, jnp.sum(product, axis=1, keepdims=True), dots)
    dots = dots.T

    shape = (rows, GROUP * rows)
    ahead = lax.broadcasted_iota(I32, shape, 0) - lax.rem(lax.broadcasted_iota(I32, shape, 1), rows)
    for kv_head in range(KVH):
        query = stacked_heads(query_ref, kv_head)
        grad = stacked_heads(residual_ref, kv_head)
        heads = range(kv_head * GROUP, (kv_head + 1) * GROUP)
        log_row = jnp.concatenate([log_ref[h : h + 1, :] for h in heads], axis=1)
        dot_row = jnp.concatenate([dots[h : h + 1, :] for h in heads], axis=1)
        key_at = slice(kv_head * DH, (kv_head + 1) * DH)
        value_at = slice(kv_width + kv_head * DH, kv_width + (kv_head + 1) * DH)

        def visit(step, query_grad):
            at = pl.ds(pl.multiple_of(step * rows, rows), rows)
            key = kv_all[at, key_at]
            value = kv_all[at, value_at]
            found = dot_f32(key, query, ((1,), (1,))) * SCALE
            weight = jnp.where(ahead <= threshold(step, z_index, x_index), jnp.exp(found - log_row), 0.0)
            grad_weight = dot_f32(value, grad, ((1,), (1,)))
            score_cot = (weight * (grad_weight - dot_row)).astype(BF16)
            part_all[at, value_at] = dot_f32(weight.astype(BF16), grad)
            part_all[at, key_at] = dot_f32(score_cot, query) * SCALE
            return query_grad + dot_f32(key.T, score_cot)

        query_grad = lax.fori_loop(0, 2 * count, visit, jnp.zeros((DH, GROUP * rows), F32))
        query_grad = query_grad * SCALE
        for h in range(GROUP):
            head = kv_head * GROUP + h
            query_out[:, head * DH : (head + 1) * DH] = query_grad[
                :, h * rows : (h + 1) * rows
            ].T.astype(BF16)
    for step in range(count):
        found = part_all[2 * step * rows : 2 * (step + 1) * rows]
        kv_outs[step][...] = found.astype(kv_outs[step].dtype)


def attend_backward(ctx, query, attended, hidden, cot, gain, inverse, log_sum, parts, kv_blocks):
    rows, width = query.shape
    count = len(kv_blocks)
    flat = jax.ShapeDtypeStruct((rows, width), BF16)
    kv_shape = (2 * rows, 2 * KVH * DH)
    result = pl.pallas_call(
        functools.partial(backward_kernel, count),
        in_specs=[SMEM] + [VMEM] * (10 + count),
        out_specs=[VMEM] * (2 + count),
        out_shape=[flat, flat]
        + [jax.ShapeDtypeStruct(kv_shape, F32)] * (count - 1)
        + [jax.ShapeDtypeStruct(kv_shape, BF16)],
        scratch_shapes=[
            pltpu.VMEM((2 * count * rows, 2 * KVH * DH), BF16),
            pltpu.VMEM((2 * count * rows, 2 * KVH * DH), F32),
        ],
        compiler_params=params(60),
        cost_estimate=cost(15),
        name="attend_backward",
    )(ctx, query, attended, hidden, cot, gain, inverse, log_sum, *parts, *kv_blocks)
    return result[0], result[1], result[2:]


def per_device(
    residual,
    query_heads,
    key_heads,
    value_heads,
    norm_gain,
    chosen_experts,
    route_weights,
    gate_weight,
    up_weight,
    down_weight,
    cotangent,
):
    rows = residual.shape[1]
    width = residual.shape[2]
    kv_width = key_heads.shape[2]
    planes = lax.axis_size("z")
    experts = planes * 8
    capacity = (9 * rows * TOPK + 8 * experts - 1) // (8 * experts)
    capacity = (capacity + 3) // 4 * 4
    z_index = lax.axis_index("z")
    x_index = lax.axis_index("x")
    y_index = lax.axis_index("y")
    core_index = lax.axis_index("core")
    groups = [list(range(first, first + STEPS)) for first in range(0, planes, STEPS)]
    names = jnp.stack(
        [
            ((z_index * 2 + (x_index ^ (chip >> 1))) * 2 + (y_index ^ (chip & 1))) * 2 + core_index
            for chip in range(4)
        ]
    ).astype(I32)
    ctx = jnp.stack([z_index, x_index]).astype(I32)
    gain = norm_gain[None, :]

    kv_own = jnp.concatenate([key_heads[0], value_heads[0]], axis=1)
    with jax.named_scope("kv_flip"):
        kv_flipped = flip_axis(kv_own, "x")
    kv_blocks = [jnp.concatenate([kv_own, kv_flipped], axis=0)]
    with jax.named_scope("kv_hop"):
        for step in range(1, planes):
            kv_blocks.append(line_up(kv_blocks[-1]))

    chosen = chosen_experts[0]
    payload = routing(chosen, route_weights[0], cotangent[0], experts)

    def gather(blocks, index, weighted, *earlier):
        sent = gather_rows(
            after(names, *earlier), blocks, metas[index], width, experts, capacity, weighted
        )
        return to_chips(sent)

    def hop(block, *earlier):
        with jax.named_scope("hop"):
            return ring_up(after(block, *earlier))

    def both_cores(block, *earlier):
        with jax.named_scope("flip"):
            return [block, flip_axis(after(block, *earlier), "core")]

    cot_pieces = []
    metas = []
    payload_blocks = []
    block = payload
    for index, group in enumerate(groups):
        for step in group:
            with jax.named_scope("cot"):
                earlier = []
                if step:
                    waits = OPT["hop"](step, kv_flipped, kv_blocks, cot_pieces)
                    block = hop(block, *waits)
                    earlier = OPT["flip"](step, kv_blocks)
                payload_blocks.append(both_cores(block, *earlier))
        metas.append(sum([payload_blocks[step] for step in group], []))
        if index == 0:
            with jax.named_scope("cot0"):
                cot_pieces.append(gather(metas[0], 0, True, *OPT["ga"](kv_blocks)))
    for index in range(1, len(groups)):
        with jax.named_scope("cot1"):
            cot_pieces.append(gather(metas[index], index, True, cot_pieces[-1][0], cot_pieces[-1][3]))
    attended, hidden, normed, inverse, log_sum = attend_forward(
        after(ctx, *OPT["att"](cot_pieces, payload_blocks)),
        query_heads[0],
        residual[0],
        gain,
        kv_blocks,
    )
    normed_blocks = []
    normed_pieces = []
    earlier = cot_pieces[-1][:3]
    block = normed
    for index, group in enumerate(groups):
        for step in group:
            with jax.named_scope("normed"):
                if step:
                    block = hop(block, *OPT["nh"](cot_pieces[-1], normed_pieces, step))
                normed_blocks.append(both_cores(block, *OPT["nf"](normed_pieces, step)))
        tokens = sum([normed_blocks[step] for step in group], [])
        with jax.named_scope("normed1" if index else "normed0"):
            normed_pieces.append(gather(tokens, index, False, *earlier))
        earlier = OPT["nb"](normed_pieces[-1]) + cot_pieces[-1][3:]
    order = normed_pieces[-1][0]
    row_pieces = []
    made_pieces = []
    for index in range(len(groups)):
        pieces = normed_pieces[index]
        waits = OPT['ea'](normed_pieces) if index == 0 else OPT['eb'](row_first)
        pieces = [after(pieces[0], order, *waits)] + pieces[1:]
        row_cot, produced = run_expert(
            pieces, cot_pieces[index], gate_weight[0], up_weight[0], down_weight[0]
        )
        order = row_cot[0]
        row_first = row_cot
        row_pieces.append(row_cot)
        made_pieces.append(produced)

    def sums(back, index, weighted, *earlier):
        own, other = combine_rows(
            after(names, *earlier), back, metas[index], width, experts, capacity, weighted
        )
        with jax.named_scope("sum_flip"):
            return own, flip_axis(other, "core")

    def term(parts, at):
        own, other = parts
        return own[at] + other[at * rows : (at + 1) * rows].astype(F32)

    row_backs = []
    row_sums = []
    for index in range(len(groups)):
        with jax.named_scope("row1" if index else "row0"):
            row_backs.append(to_chips(gated(row_pieces[index], *OPT['row1'](row_backs))))
    for index in range(len(groups)):
        with jax.named_scope("row1" if index else "row0"):
            later = [first_moved] if index else OPT['ca'](row_backs)
            row_sums.append(sums(row_backs[index], index, False, order, *later))
        if index == 0:
            total = term(row_sums[0], 1).astype(BF16)
            with jax.named_scope("row_hop"):
                first_moved = ring_up(total)
        order = row_sums[-1][0][0]

    made_backs = [None] * len(groups)
    made_sums = [None] * len(groups)
    earlier = row_backs[-1]
    for index in reversed(range(len(groups))):
        with jax.named_scope("made1" if index else "made0"):
            made_backs[index] = to_chips(gated(made_pieces[index], *earlier[1:]))
        earlier = made_backs[index]

    with jax.named_scope("row_hop"):
        for step in range(2, planes):
            if step == 2:
                moved = first_moved
            else:
                moved = ring_up(after(total, *OPT['hop2'](made_backs[-1])))
            total = moved.astype(F32) + term(row_sums[step // STEPS], step % STEPS)
            total = total.astype(BF16)
        cot_terms = (ring_up(total), row_sums[0][0][0], row_sums[0][1])
    for index in reversed(range(1, len(groups))):
        with jax.named_scope("made1"):
            made_sums[index] = sums(made_backs[index], index, True, cot_terms[0])

    residual_gradient, query_gradient, kv_parts = attend_backward(
        after(ctx, made_sums[1][0][0], *OPT['attb'](made_backs[0])),
        query_heads[0],
        attended,
        hidden,
        cotangent[0],
        gain,
        inverse,
        log_sum,
        cot_terms,
        kv_blocks,
    )
    kv_total = kv_parts[-1]
    kv_low = []
    for step in reversed(range(1, planes - 1)):
        with jax.named_scope("kv_back_hop"):
            kv_total = line_down(kv_total)
        kv_total = (kv_total.astype(F32) + kv_parts[step]).astype(BF16)
        kv_low.append(kv_total)

    made_total = None
    for step in reversed(range(STEPS, planes)):
        part = term(made_sums[step // STEPS], step % STEPS)
        with jax.named_scope("made_hop"):
            if made_total is not None:
                part = after(made_total, kv_low[0]).astype(F32) + part
            made_total = ring_down(part.astype(BF16))
    with jax.named_scope("made0"):
        made_sums[0] = sums(made_backs[0], 0, True, *kv_low, made_total)
    for step in reversed(range(STEPS)):
        moe_sum = made_total.astype(F32) + term(made_sums[0], step)
        if step:
            moved = moe_sum.astype(BF16)
            with jax.named_scope("made_hop"):
                made_total = ring_down(moved)
            with jax.named_scope("kv_back_hop"):
                kv_total = line_down(kv_total)
            kv_total = kv_total.astype(F32) + kv_parts[0]
            with jax.named_scope("kv_back_flip"):
                kv_flipped_total = flip_axis(
                    after(kv_total[rows:].astype(BF16), made_total), "x"
                )
            kv_total = (kv_total[:rows] + kv_flipped_total.astype(F32)).astype(BF16)
    key_gradient = kv_total[:, :kv_width]
    value_gradient = kv_total[:, kv_width:]
    layer_out = (hidden.astype(F32) + moe_sum[:, :width]).astype(BF16)

    found = moe_sum[:, width:].reshape(rows, 4, experts)
    found = found[:, 0] + found[:, 1] + found[:, 2]
    hits = chosen[:, :, None] == jnp.arange(experts, dtype=I32)
    route_dot = jnp.sum(jnp.where(hits, found[:, None, :], 0.0), axis=2)
    share_raw = route_weights[0]
    route_total = jnp.sum(share_raw, axis=1, keepdims=True)
    route_share = share_raw / route_total
    route_gradient = (
        route_dot - jnp.sum(route_share * route_dot, axis=1, keepdims=True)
    ) / route_total
    return (
        layer_out[None],
        residual_gradient[None],
        query_gradient[None],
        key_gradient[None],
        value_gradient[None],
        route_gradient[None],
    )


def solution(mesh):
    fine = Mesh(
        mesh.devices.reshape(mesh.shape["ctx"] // 2, 2, mesh.shape["exp"] // 2, 2),
        ("z", "x", "y", "core"),
    )
    tokens = P(("y", "core"), ("z", "x"), None)
    expert = P(("z", "x", "y", "core"), None, None)
    return jax.shard_map(
        per_device,
        mesh=fine,
        in_specs=(tokens,) * 4 + (P(),) + (tokens,) * 2 + (expert,) * 3 + (tokens,),
        out_specs=(tokens,) * 6,
        check_vma=False,
    )
```

```python
import functools

import jax
import jax.numpy as jnp
from jax import lax
from jax.experimental import pallas as pl
from jax.experimental.pallas import tpu as pltpu
from jax.sharding import Mesh, PartitionSpec as P

H = 16
KVH = 2
DH = 128
TOPK = 8
GROUP = H // KVH
STEPS = 2

NEG = -1e30
OPT = {
    "att": lambda cot, blocks: [cot[-1][0]],
    "hop": lambda step, flipped, kv, cot: {1: [flipped], 3: cot[0][1:3] + [kv[2]] if cot else []}.get(step, []),
    "flip": lambda step, kv: {1: [kv[1]], 3: kv[3:4]}.get(step, []),
    "ga": lambda kv: [],
    "nh": lambda cot, normed, step: {2: cot[1:3], 3: cot[3:] + normed[0][:1] if normed else []}.get(step, []),
    "nf": lambda normed, step: normed[0][1:3] if step == 2 else [],
    "nb": lambda normed: normed[:4],
    "hb": lambda arrivals: [arrivals[0]],
    "ea": lambda normed: [],
    "eb": lambda rows: [],
    "row1": lambda backs: [],
    "ca": lambda backs: [],
    "attb": lambda back: [],
    "hop2": lambda back: [],
}
EPSILON = 1e-06
SCALE = DH ** (-0.5)
F32 = jnp.float32
BF16 = jnp.bfloat16
I32 = jnp.int32
SMEM = pl.BlockSpec(memory_space=pltpu.SMEM)
VMEM = pl.BlockSpec(memory_space=pltpu.VMEM)
MIB = 1 << 20


def dot_f32(a, b, dims=((1,), (0,))):
    return lax.dot_general(a, b, (dims, ((), ())), preferred_element_type=F32)


def flip_axis(value, name):
    return lax.ppermute(value, name, [(0, 1), (1, 0)])


def flip_xy(value):
    return lax.ppermute(value, ("x", "y"), [(i, 3 - i) for i in range(4)])


def ring_up(value):
    size = lax.axis_size("z")
    return lax.ppermute(value, "z", [(i, (i + 1) % size) for i in range(size)])


def line_up(value):
    size = lax.axis_size("z")
    return lax.ppermute(value, "z", [(i, i + 1) for i in range(size - 1)])


def line_down(value):
    size = lax.axis_size("z")
    return lax.ppermute(value, "z", [(i + 1, i) for i in range(size - 1)])


def ring_down(value):
    size = lax.axis_size("z")
    return lax.ppermute(value, "z", [(i, (i - 1) % size) for i in range(size)])


def to_chips(blocks):
    with jax.named_scope("to_y"):
        to_y = flip_axis(blocks[1], "y")
    with jax.named_scope("to_x"):
        to_x = flip_axis(blocks[2], "x")
    with jax.named_scope("to_xy"):
        to_xy = flip_xy(blocks[3])
    return [blocks[0], to_y, to_x, to_xy]


def params(mib):
    return pltpu.CompilerParams(vmem_limit_bytes=mib * MIB)


def cost(microseconds):
    return pl.CostEstimate(flops=0, bytes_accessed=int(microseconds * 1e6), transcendentals=0)


def gated(values, *others):
    return lax.optimization_barrier((*values, *others))[: len(values)]


def after(value, *others):
    return lax.optimization_barrier((value,) + others)[0]


def routing_kernel(experts, chosen_ref, raw_ref, cot_ref, payload_ref):
    rows, width = cot_ref.shape
    chosen = chosen_ref[...]
    raw = raw_ref[...]
    share = raw / jnp.sum(raw, axis=0, keepdims=True)
    names = lax.broadcasted_iota(I32, (experts, rows), 0)
    hit = jnp.zeros((experts, rows), F32)
    table = jnp.zeros((experts, rows), F32)
    for k in range(TOPK):
        here = names == chosen[k : k + 1]
        hit = hit + jnp.where(here, 1.0, 0.0)
        table = table + jnp.where(here, share[k : k + 1], 0.0)
    before = lax.broadcasted_iota(I32, (rows, rows), 0) < lax.broadcasted_iota(I32, (rows, rows), 1)
    earlier = dot_f32(hit.astype(BF16), jnp.where(before, 1.0, 0.0).astype(BF16))
    slots = jnp.where(hit > 0.5, earlier, -1.0)
    high = table.astype(BF16).astype(F32)
    middle = (table - high).astype(BF16).astype(F32)
    low = table - high - middle
    meta = jnp.concatenate([slots, high, middle, low], axis=0).astype(BF16)
    payload_ref[:, :width] = cot_ref[...]
    for block in range(4 * experts // rows):
        payload_ref[:, width + block * rows : width + (block + 1) * rows] = meta[
            block * rows : (block + 1) * rows
        ]


def routing(chosen, raw, cotangent, experts):
    rows, width = cotangent.shape
    return pl.pallas_call(
        functools.partial(routing_kernel, experts),
        in_specs=[VMEM] * 3,
        out_specs=VMEM,
        out_shape=jax.ShapeDtypeStruct((rows, width + 4 * experts), BF16),
        compiler_params=params(16),
        cost_estimate=cost(3),
        name="routing",
    )(chosen.T, raw.T, cotangent)


def table_row(meta, kind, experts, expert):
    rows = meta.shape[0]
    block, offset = divmod(kind * experts, rows)
    part = meta[:, block * rows : (block + 1) * rows].astype(F32)[offset : offset + experts]
    here = lax.broadcasted_iota(I32, part.shape, 0) == expert
    return jnp.sum(jnp.where(here, part, 0.0), axis=0, keepdims=True)


def table_column(meta_turned, kind, experts, expert):
    rows = meta_turned[0].shape[0]
    block, offset = divmod(kind * experts, rows)
    part = meta_turned[block]
    here = lax.broadcasted_iota(I32, part.shape, 1) == expert + offset
    return jnp.sum(jnp.where(here, part, 0.0), axis=1, keepdims=True)


def gather_kernel(experts, capacity, weighted, blocks, names_ref, *refs):
    token_refs = refs[:blocks]
    meta_refs = refs[blocks : 2 * blocks]
    out_refs = refs[2 * blocks : 2 * blocks + 4]
    pick_all, share_all = refs[2 * blocks + 4 :]
    sent_rows = out_refs[0].shape[0]
    rows = token_refs[0].shape[0]

    @pl.when(pl.program_id(0) == 0)
    def _():
        metas = [ref[...] for ref in meta_refs]
        places = lax.broadcasted_iota(I32, (sent_rows, rows), 0)
        for chip in range(4):
            expert = names_ref[chip]
            share = jnp.zeros((sent_rows, rows), F32)
            for which, meta in enumerate(metas):
                slot = table_row(meta, 0, experts, expert)
                target = jnp.where(slot >= 0, slot + which * capacity, -1.0).astype(I32)
                pick = places == target
                if weighted:
                    row = (
                        table_row(meta, 1, experts, expert)
                        + table_row(meta, 2, experts, expert)
                        + table_row(meta, 3, experts, expert)
                    )
                    share = share + jnp.where(pick, row, 0.0)
                pick_all[chip, :, which * rows : (which + 1) * rows] = jnp.where(
                    pick, 1.0, 0.0
                ).astype(BF16)
            if weighted:
                share_all[chip] = jnp.sum(share, axis=1, keepdims=True)

    tokens = jnp.concatenate([ref[...] for ref in token_refs], axis=0)
    for chip in range(4):
        found = dot_f32(pick_all[chip], tokens)
        if weighted:
            found = found * share_all[chip]
        out_refs[chip][...] = found.astype(BF16)


def gather_rows(names, token_blocks, meta_blocks, width, experts, capacity, weighted):
    rows = token_blocks[0].shape[0]
    blocks = len(token_blocks)
    sent_rows = blocks * capacity
    meta_width = 4 * experts
    cut = 512
    return pl.pallas_call(
        functools.partial(gather_kernel, experts, capacity, weighted, blocks),
        grid=(width // cut,),
        in_specs=[SMEM]
        + [pl.BlockSpec((rows, cut), lambda c: (0, c))] * blocks
        + [pl.BlockSpec((rows, meta_width), lambda c: (0, width // meta_width))] * blocks,
        out_specs=[pl.BlockSpec((sent_rows, cut), lambda c: (0, c))] * 4,
        out_shape=[jax.ShapeDtypeStruct((sent_rows, width), BF16)] * 4,
        scratch_shapes=[
            pltpu.VMEM((4, sent_rows, blocks * rows), BF16),
            pltpu.VMEM((4, sent_rows, 1), F32),
        ],
        compiler_params=params(32),
        cost_estimate=cost(4),
        name="gather_weighted" if weighted else "gather_plain",
    )(names, *token_blocks, *meta_blocks)


def expert_kernel(*refs):
    normed_refs = refs[0:4]
    cot_refs = refs[4:8]
    weight_refs = refs[8:11]
    row_refs = refs[11:15]
    made_refs = refs[15:19]
    gate, up, down, normed_all, cot_all, row_all, made_all, in_sem, weight_sem, out_sem = refs[19:]
    piece = normed_refs[0].shape[0]
    half = 2 * piece

    def place(chip):
        return pl.ds(chip * piece, piece)

    normed_in = [
        pltpu.make_async_copy(normed_refs[c], normed_all.at[place(c)], in_sem.at[0, c])
        for c in range(4)
    ]
    cot_in = [
        pltpu.make_async_copy(cot_refs[c], cot_all.at[place(c)], in_sem.at[1, c]) for c in range(4)
    ]
    weight_in = [
        pltpu.make_async_copy(weight_refs[w], held, weight_sem.at[w])
        for w, held in enumerate((gate, up, down))
    ]
    for copy in normed_in[:2] + weight_in[:2] + cot_in[:2] + weight_in[2:]:
        copy.start()
    for copy in normed_in[2:] + cot_in[2:]:
        copy.start()
    copies_out = []
    for part in range(2):
        chips = (2 * part, 2 * part + 1)
        rows = pl.ds(part * half, half)
        for c in chips:
            normed_in[c].wait()
        if part == 0:
            weight_in[0].wait()
        gate_act = dot_f32(normed_all[rows], gate[...])
        if part == 0:
            weight_in[1].wait()
        up_act = dot_f32(normed_all[rows], up[...])
        for c in chips:
            cot_in[c].wait()
        if part == 0:
            weight_in[2].wait()
        act_cot = dot_f32(cot_all[rows], down[...], ((1,), (1,)))
        sigma = jax.nn.sigmoid(gate_act)
        silu = gate_act * sigma
        gate_cot = (act_cot * up_act * sigma * (1.0 + gate_act * (1.0 - sigma))).astype(BF16)
        up_cot = (act_cot * silu).astype(BF16)
        activation = (silu * up_act).astype(BF16)
        row_all[rows] = (
            dot_f32(gate_cot, gate[...], ((1,), (1,))) + dot_f32(up_cot, up[...], ((1,), (1,)))
        ).astype(BF16)
        for c in chips:
            copy = pltpu.make_async_copy(row_all.at[place(c)], row_refs[c], out_sem.at[0, c])
            copy.start()
            copies_out.append(copy)
        made_all[rows] = dot_f32(activation, down[...]).astype(BF16)
        for c in chips:
            copy = pltpu.make_async_copy(made_all.at[place(c)], made_refs[c], out_sem.at[1, c])
            copy.start()
            copies_out.append(copy)
    for copy in copies_out:
        copy.wait()


def run_expert(normed_pieces, cot_pieces, gate_mat, up_mat, down_mat):
    piece, width = normed_pieces[0].shape
    anywhere = pl.BlockSpec(memory_space=pl.ANY)
    everything = pltpu.VMEM((4 * piece, width), BF16)
    result = pl.pallas_call(
        expert_kernel,
        in_specs=[anywhere] * 11,
        out_specs=[anywhere] * 8,
        out_shape=[jax.ShapeDtypeStruct((piece, width), BF16)] * 8,
        scratch_shapes=[
            pltpu.VMEM(gate_mat.shape, BF16),
            pltpu.VMEM(up_mat.shape, BF16),
            pltpu.VMEM(down_mat.shape, BF16),
        ]
        + [everything] * 4
        + [
            pltpu.SemaphoreType.DMA((2, 4)),
            pltpu.SemaphoreType.DMA((3,)),
            pltpu.SemaphoreType.DMA((2, 4)),
        ],
        compiler_params=params(60),
        cost_estimate=cost(18),
        name="expert",
    )(*normed_pieces, *cot_pieces, gate_mat, up_mat, down_mat)
    return result[0:4], result[4:8]


def combine_kernel(experts, capacity, blocks, names_ref, *refs):
    back_refs = refs[:4]
    meta_refs = refs[4 : 4 + blocks]
    own_refs = refs[4 + blocks : 4 + blocks + blocks // 2]
    other_ref = refs[4 + blocks + blocks // 2]
    pick_all = refs[5 + blocks + blocks // 2]

    @pl.when(pl.program_id(0) == 0)
    def _():
        fill_picks(
            experts, capacity, False, names_ref, back_refs[0].shape[0], meta_refs, pick_all
        )

    rows = meta_refs[0].shape[0]
    total = dot_f32(pick_all[...], jnp.concatenate([ref[...] for ref in back_refs], axis=0))
    for which in range(blocks):
        part = total[which * rows : (which + 1) * rows]
        if which % 2 == 0:
            own_refs[which // 2][...] = part
        else:
            other_ref[which // 2 * rows : (which // 2 + 1) * rows] = part.astype(BF16)


def fill_picks(experts, capacity, weighted, names_ref, piece, meta_refs, pick_all):
    rows = meta_refs[0].shape[0]
    places = lax.broadcasted_iota(I32, (rows, 4 * piece), 1)
    for which, meta_ref in enumerate(meta_refs):
        meta = meta_ref[...].astype(F32)
        turned = [meta[:, b * rows : (b + 1) * rows].T for b in range(meta.shape[1] // rows)]
        pick = jnp.zeros((rows, 4 * piece), F32)
        for chip in range(4):
            expert = names_ref[chip]
            slot = table_column(turned, 0, experts, expert)
            target = jnp.where(slot >= 0, slot + (which * capacity + chip * piece), -1.0)
            here = places == target.astype(I32)
            value = table_column(turned, 1, experts, expert) if weighted else 1.0
            pick = jnp.where(here, value, pick)
        pick_all[which * rows : (which + 1) * rows] = pick.astype(BF16)


def weighted_kernel(experts, capacity, blocks, names_ref, *refs):
    back_refs = refs[:4]
    meta_refs = refs[4 : 4 + blocks]
    cot_refs = refs[4 + blocks : 4 + 2 * blocks]
    own_refs = refs[4 + 2 * blocks : 4 + 2 * blocks + blocks // 2]
    other_ref, pick_all, dots_all = refs[4 + 2 * blocks + blocks // 2 :]
    piece, cut = back_refs[0].shape
    rows = meta_refs[0].shape[0]
    step = pl.program_id(0)

    @pl.when(step == 0)
    def _():
        fill_picks(experts, capacity, True, names_ref, piece, meta_refs, pick_all)
        dots_all[...] = jnp.zeros_like(dots_all)

    back = jnp.concatenate([ref[...] for ref in back_refs], axis=0)
    cots = jnp.concatenate([ref[...] for ref in cot_refs], axis=0)
    dots_all[...] += dot_f32(cots, back, ((1,), (1,)))
    total = dot_f32(pick_all[...], back)
    at = pl.ds(pl.multiple_of(step * cut, cut), cut)
    for which in range(blocks):
        part = total[which * rows : (which + 1) * rows]
        if which % 2 == 0:
            own_refs[which // 2][:, at] = part
        else:
            other_ref[which // 2 * rows : (which // 2 + 1) * rows, at] = part.astype(BF16)

    @pl.when(step == pl.num_programs(0) - 1)
    def _():
        width = other_ref.shape[1] - 4 * experts
        places = lax.broadcasted_iota(I32, (rows, 4 * piece), 1)
        lane = lax.broadcasted_iota(I32, (rows, 4 * experts), 1)
        for which in range(blocks):
            found = dots_all[which * rows : (which + 1) * rows]
            picked = pick_all[which * rows : (which + 1) * rows].astype(F32) > 0
            found = jnp.where(picked, found, 0.0)
            tail = jnp.zeros((rows, 4 * experts), F32)
            for chip in range(4):
                here = (places >= chip * piece) & (places < (chip + 1) * piece)
                value = jnp.sum(jnp.where(here, found, 0.0), axis=1, keepdims=True)
                for part in range(3):
                    low = value.astype(BF16).astype(F32)
                    tail = jnp.where(lane == names_ref[chip] + part * experts, low, tail)
                    value = value - low
            if which % 2 == 0:
                own_refs[which // 2][:, width:] = tail
            else:
                other_ref[which // 2 * rows : (which // 2 + 1) * rows, width:] = tail.astype(BF16)


def combine_rows(names, back, metas, width, experts, capacity, weighted):
    piece = back[0].shape[0]
    rows = metas[0].shape[0]
    blocks = len(metas)
    meta_width = 4 * experts
    cut = 512
    chunks = [pl.BlockSpec((piece, cut), lambda c: (0, c))] * 4
    metas_in = [pl.BlockSpec((rows, meta_width), lambda c: (0, width // meta_width))] * blocks
    if weighted:
        kernel = weighted_kernel
        metas_in = metas_in + [pl.BlockSpec((rows, cut), lambda c: (0, c))] * blocks
        metas = metas + metas
        width_out = width + meta_width
        own_spec = pl.BlockSpec((rows, width_out), lambda c: (0, 0))
        other_spec = pl.BlockSpec((blocks // 2 * rows, width_out), lambda c: (0, 0))
        scratch = [
            pltpu.VMEM((blocks * rows, 4 * piece), BF16),
            pltpu.VMEM((blocks * rows, 4 * piece), F32),
        ]
    else:
        kernel = combine_kernel
        width_out = width
        own_spec = pl.BlockSpec((rows, cut), lambda c: (0, c))
        other_spec = pl.BlockSpec((blocks // 2 * rows, cut), lambda c: (0, c))
        scratch = [pltpu.VMEM((blocks * rows, 4 * piece), BF16)]
    result = pl.pallas_call(
        functools.partial(kernel, experts, capacity, blocks),
        grid=(width // cut,),
        in_specs=[SMEM] + chunks + metas_in,
        out_specs=[own_spec] * (blocks // 2) + [other_spec],
        out_shape=[jax.ShapeDtypeStruct((rows, width_out), F32)] * (blocks // 2)
        + [jax.ShapeDtypeStruct((blocks // 2 * rows, width_out), BF16)],
        scratch_shapes=scratch,
        compiler_params=params(32),
        cost_estimate=cost(8),
        name="combine_weighted" if weighted else "combine_plain",
    )(names, *back, *metas)
    return result[:-1], result[-1]


def threshold(step, z_index, x_index):
    lower = jnp.where(step == 1, x_index == 1, step // 2 <= z_index)
    return jnp.where(step == 0, 0, jnp.where(lower, DH * 1024, -DH * 1024))


def stacked_heads(ref, kv_head):
    first = kv_head * GROUP
    return jnp.concatenate(
        [ref[:, (first + h) * DH : (first + h + 1) * DH] for h in range(GROUP)], axis=0
    )


def forward_kernel(count, ctx_ref, query_ref, residual_ref, gain_ref, *refs):
    kv_refs = refs[:count]
    attended_ref, hidden_ref, normed_ref, inverse_ref, log_ref = refs[count : count + 5]
    kv_all, score_all = refs[count + 5 :]
    rows = query_ref.shape[0]
    kv_width = KVH * DH
    for step in range(count):
        kv_all[2 * step * rows : (2 * step + 2) * rows] = kv_refs[step][...]
    z_index = ctx_ref[0]
    x_index = ctx_ref[1]
    shape = (rows, GROUP * rows)
    ahead = lax.broadcasted_iota(I32, shape, 0) - lax.rem(lax.broadcasted_iota(I32, shape, 1), rows)
    for kv_head in range(KVH):
        query = stacked_heads(query_ref, kv_head)

        def score(step, top):
            at = pl.ds(pl.multiple_of(step * rows, rows), rows)
            key = kv_all[at, kv_head * DH : (kv_head + 1) * DH]
            found = dot_f32(key, query, ((1,), (1,))) * SCALE
            found = jnp.where(ahead <= threshold(step, z_index, x_index), found, NEG)
            score_all[at] = found
            return jnp.maximum(top, jnp.max(found, axis=0, keepdims=True))

        top = lax.fori_loop(0, 2 * count, score, jnp.full((1, GROUP * rows), NEG, F32))

        def gather_values(step, state):
            total, mixed = state
            at = pl.ds(pl.multiple_of(step * rows, rows), rows)
            weight = jnp.exp(score_all[at] - top)
            value = kv_all[at, kv_width + kv_head * DH : kv_width + (kv_head + 1) * DH]
            total = total + jnp.sum(weight, axis=0, keepdims=True)
            mixed = mixed + dot_f32(value.T, weight.astype(BF16))
            return total, mixed

        total, mixed = lax.fori_loop(
            0,
            2 * count,
            gather_values,
            (jnp.zeros((1, GROUP * rows), F32), jnp.zeros((DH, GROUP * rows), F32)),
        )
        mixed = mixed / total
        log_sum = top + jnp.log(total)
        for h in range(GROUP):
            head = kv_head * GROUP + h
            at = slice(h * rows, (h + 1) * rows)
            attended_ref[:, head * DH : (head + 1) * DH] = mixed[:, at].T.astype(BF16)
            log_ref[head : head + 1, :] = log_sum[:, at]
    hidden = (residual_ref[...].astype(F32) + attended_ref[...].astype(F32)).astype(BF16)
    hidden_ref[...] = hidden
    wide = hidden.astype(F32)
    inverse = lax.rsqrt(jnp.mean(wide * wide, axis=1, keepdims=True) + EPSILON)
    inverse_ref[...] = inverse
    normed_ref[...] = (wide * inverse * gain_ref[...]).astype(BF16)


def attend_forward(ctx, query, residual, gain, kv_blocks):
    rows, width = query.shape
    count = len(kv_blocks)
    flat = jax.ShapeDtypeStruct((rows, width), BF16)
    return pl.pallas_call(
        functools.partial(forward_kernel, count),
        in_specs=[SMEM] + [VMEM] * (3 + count),
        out_specs=[VMEM] * 5,
        out_shape=[
            flat,
            flat,
            flat,
            jax.ShapeDtypeStruct((rows, 1), F32),
            jax.ShapeDtypeStruct((H, rows), F32),
        ],
        scratch_shapes=[
            pltpu.VMEM((2 * count * rows, 2 * KVH * DH), BF16),
            pltpu.VMEM((2 * count * rows, GROUP * rows), F32),
        ],
        compiler_params=params(60),
        cost_estimate=cost(12),
        name="attend_forward",
    )(ctx, query, residual, gain, *kv_blocks)


def backward_kernel(count, ctx_ref, *refs):
    (query_ref, attended_ref, hidden_ref, cot_ref, gain_ref, inverse_ref, log_ref) = refs[:7]
    ring_ref, own_ref, other_ref = refs[7:10]
    kv_refs = refs[10 : 10 + count]
    residual_ref, query_out = refs[10 + count : 12 + count]
    kv_outs = refs[12 + count : 12 + 2 * count]
    kv_all, part_all = refs[12 + 2 * count :]
    rows = query_ref.shape[0]
    kv_width = KVH * DH
    for step in range(count):
        kv_all[2 * step * rows : (2 * step + 2) * rows] = kv_refs[step][...]
    z_index = ctx_ref[0]
    x_index = ctx_ref[1]

    normed_cot = ring_ref[...].astype(F32) + own_ref[...] + other_ref[:rows].astype(F32)
    gained = gain_ref[...] * normed_cot
    hidden = hidden_ref[...].astype(F32)
    inverse = inverse_ref[...]
    mean = jnp.mean(hidden * gained, axis=1, keepdims=True)
    hidden_cot = inverse * gained - hidden * (inverse * inverse * inverse) * mean
    residual_ref[...] = (cot_ref[...].astype(F32) + hidden_cot).astype(BF16)

    lane = lax.broadcasted_iota(I32, (rows, DH), 1)
    dots = jnp.zeros((rows, DH), F32)
    for head in range(H):
        at = slice(head * DH, (head + 1) * DH)
        product = residual_ref[:, at].astype(F32) * attended_ref[:, at].astype(F32)
        dots = jnp.where(lane == head, jnp.sum(product, axis=1, keepdims=True), dots)
    dots = dots.T

    shape = (rows, GROUP * rows)
    ahead = lax.broadcasted_iota(I32, shape, 0) - lax.rem(lax.broadcasted_iota(I32, shape, 1), rows)
    for kv_head in range(KVH):
        query = stacked_heads(query_ref, kv_head)
        grad = stacked_heads(residual_ref, kv_head)
        heads = range(kv_head * GROUP, (kv_head + 1) * GROUP)
        log_row = jnp.concatenate([log_ref[h : h + 1, :] for h in heads], axis=1)
        dot_row = jnp.concatenate([dots[h : h + 1, :] for h in heads], axis=1)
        key_at = slice(kv_head * DH, (kv_head + 1) * DH)
        value_at = slice(kv_width + kv_head * DH, kv_width + (kv_head + 1) * DH)

        def visit(step, query_grad):
            at = pl.ds(pl.multiple_of(step * rows, rows), rows)
            key = kv_all[at, key_at]
            value = kv_all[at, value_at]
            found = dot_f32(key, query, ((1,), (1,))) * SCALE
            weight = jnp.where(ahead <= threshold(step, z_index, x_index), jnp.exp(found - log_row), 0.0)
            grad_weight = dot_f32(value, grad, ((1,), (1,)))
            score_cot = (weight * (grad_weight - dot_row)).astype(BF16)
            part_all[at, value_at] = dot_f32(weight.astype(BF16), grad)
            part_all[at, key_at] = dot_f32(score_cot, query) * SCALE
            return query_grad + dot_f32(key.T, score_cot)

        query_grad = lax.fori_loop(0, 2 * count, visit, jnp.zeros((DH, GROUP * rows), F32))
        query_grad = query_grad * SCALE
        for h in range(GROUP):
            head = kv_head * GROUP + h
            query_out[:, head * DH : (head + 1) * DH] = query_grad[
                :, h * rows : (h + 1) * rows
            ].T.astype(BF16)
    for step in range(count):
        found = part_all[2 * step * rows : 2 * (step + 1) * rows]
        kv_outs[step][...] = found.astype(kv_outs[step].dtype)


def attend_backward(ctx, query, attended, hidden, cot, gain, inverse, log_sum, parts, kv_blocks):
    rows, width = query.shape
    count = len(kv_blocks)
    flat = jax.ShapeDtypeStruct((rows, width), BF16)
    kv_shape = (2 * rows, 2 * KVH * DH)
    result = pl.pallas_call(
        functools.partial(backward_kernel, count),
        in_specs=[SMEM] + [VMEM] * (10 + count),
        out_specs=[VMEM] * (2 + count),
        out_shape=[flat, flat]
        + [jax.ShapeDtypeStruct(kv_shape, F32)] * (count - 1)
        + [jax.ShapeDtypeStruct(kv_shape, BF16)],
        scratch_shapes=[
            pltpu.VMEM((2 * count * rows, 2 * KVH * DH), BF16),
            pltpu.VMEM((2 * count * rows, 2 * KVH * DH), F32),
        ],
        compiler_params=params(60),
        cost_estimate=cost(15),
        name="attend_backward",
    )(ctx, query, attended, hidden, cot, gain, inverse, log_sum, *parts, *kv_blocks)
    return result[0], result[1], result[2:]


def per_device(
    residual,
    query_heads,
    key_heads,
    value_heads,
    norm_gain,
    chosen_experts,
    route_weights,
    gate_weight,
    up_weight,
    down_weight,
    cotangent,
):
    rows = residual.shape[1]
    width = residual.shape[2]
    kv_width = key_heads.shape[2]
    planes = lax.axis_size("z")
    experts = planes * 8
    capacity = (9 * rows * TOPK + 8 * experts - 1) // (8 * experts)
    capacity = (capacity + 3) // 4 * 4
    z_index = lax.axis_index("z")
    x_index = lax.axis_index("x")
    y_index = lax.axis_index("y")
    core_index = lax.axis_index("core")
    groups = [list(range(first, first + STEPS)) for first in range(0, planes, STEPS)]
    names = jnp.stack(
        [
            ((z_index * 2 + (x_index ^ (chip >> 1))) * 2 + (y_index ^ (chip & 1))) * 2 + core_index
            for chip in range(4)
        ]
    ).astype(I32)
    ctx = jnp.stack([z_index, x_index]).astype(I32)
    gain = norm_gain[None, :]

    kv_own = jnp.concatenate([key_heads[0], value_heads[0]], axis=1)
    with jax.named_scope("kv_flip"):
        kv_flipped = flip_axis(kv_own, "x")
    kv_blocks = [jnp.concatenate([kv_own, kv_flipped], axis=0)]
    with jax.named_scope("kv_hop"):
        for step in range(1, planes):
            kv_blocks.append(line_up(kv_blocks[-1]))

    chosen = chosen_experts[0]
    payload = routing(chosen, route_weights[0], cotangent[0], experts)

    def gather(blocks, index, weighted, *earlier):
        sent = gather_rows(
            after(names, *earlier), blocks, metas[index], width, experts, capacity, weighted
        )
        return to_chips(sent)

    def hop(block, *earlier):
        with jax.named_scope("hop"):
            return ring_up(after(block, *earlier))

    def both_cores(block, *earlier):
        with jax.named_scope("flip"):
            return [block, flip_axis(after(block, *earlier), "core")]

    cot_pieces = []
    metas = []
    payload_blocks = []
    block = payload
    for index, group in enumerate(groups):
        for step in group:
            with jax.named_scope("cot"):
                earlier = []
                if step:
                    waits = OPT["hop"](step, kv_flipped, kv_blocks, cot_pieces)
                    block = hop(block, *waits)
                    earlier = OPT["flip"](step, kv_blocks)
                payload_blocks.append(both_cores(block, *earlier))
        metas.append(sum([payload_blocks[step] for step in group], []))
        if index == 0:
            with jax.named_scope("cot0"):
                cot_pieces.append(gather(metas[0], 0, True, *OPT["ga"](kv_blocks)))
    for index in range(1, len(groups)):
        with jax.named_scope("cot1"):
            cot_pieces.append(gather(metas[index], index, True, cot_pieces[-1][0], cot_pieces[-1][3]))
    attended, hidden, normed, inverse, log_sum = attend_forward(
        after(ctx, *OPT["att"](cot_pieces, payload_blocks)),
        query_heads[0],
        residual[0],
        gain,
        kv_blocks,
    )
    normed_blocks = []
    normed_pieces = []
    earlier = cot_pieces[-1][:3]
    block = normed
    for index, group in enumerate(groups):
        for step in group:
            with jax.named_scope("normed"):
                if step:
                    block = hop(block, *OPT["nh"](cot_pieces[-1], normed_pieces, step))
                normed_blocks.append(both_cores(block, *OPT["nf"](normed_pieces, step)))
        tokens = sum([normed_blocks[step] for step in group], [])
        with jax.named_scope("normed1" if index else "normed0"):
            normed_pieces.append(gather(tokens, index, False, *earlier))
        earlier = OPT["nb"](normed_pieces[-1]) + cot_pieces[-1][3:]
    order = normed_pieces[-1][0]
    row_pieces = []
    made_pieces = []
    for index in range(len(groups)):
        pieces = normed_pieces[index]
        waits = OPT['ea'](normed_pieces) if index == 0 else OPT['eb'](row_first)
        pieces = [after(pieces[0], order, *waits)] + pieces[1:]
        row_cot, produced = run_expert(
            pieces, cot_pieces[index], gate_weight[0], up_weight[0], down_weight[0]
        )
        order = row_cot[0]
        row_first = row_cot
        row_pieces.append(row_cot)
        made_pieces.append(produced)

    def sums(back, index, weighted, *earlier):
        own, other = combine_rows(
            after(names, *earlier), back, metas[index], width, experts, capacity, weighted
        )
        with jax.named_scope("sum_flip"):
            return own, flip_axis(other, "core")

    def term(parts, at):
        own, other = parts
        return own[at] + other[at * rows : (at + 1) * rows].astype(F32)

    row_backs = []
    row_sums = []
    for index in range(len(groups)):
        with jax.named_scope("row1" if index else "row0"):
            row_backs.append(to_chips(gated(row_pieces[index], *OPT['row1'](row_backs))))
    for index in range(len(groups)):
        with jax.named_scope("row1" if index else "row0"):
            later = [first_moved] if index else OPT['ca'](row_backs)
            row_sums.append(sums(row_backs[index], index, False, order, *later))
        if index == 0:
            total = term(row_sums[0], 1).astype(BF16)
            with jax.named_scope("row_hop"):
                first_moved = ring_up(total)
        order = row_sums[-1][0][0]

    made_backs = [None] * len(groups)
    made_sums = [None] * len(groups)
    earlier = row_backs[-1]
    for index in reversed(range(len(groups))):
        with jax.named_scope("made1" if index else "made0"):
            made_backs[index] = to_chips(gated(made_pieces[index], *earlier[1:]))
        earlier = made_backs[index]

    with jax.named_scope("row_hop"):
        for step in range(2, planes):
            if step == 2:
                moved = first_moved
            else:
                moved = ring_up(after(total, *OPT['hop2'](made_backs[-1])))
            total = moved.astype(F32) + term(row_sums[step // STEPS], step % STEPS)
            total = total.astype(BF16)
        cot_terms = (ring_up(total), row_sums[0][0][0], row_sums[0][1])
    for index in reversed(range(1, len(groups))):
        with jax.named_scope("made1"):
            made_sums[index] = sums(made_backs[index], index, True, cot_terms[0])

    residual_gradient, query_gradient, kv_parts = attend_backward(
        after(ctx, made_sums[1][0][0], *OPT['attb'](made_backs[0])),
        query_heads[0],
        attended,
        hidden,
        cotangent[0],
        gain,
        inverse,
        log_sum,
        cot_terms,
        kv_blocks,
    )
    kv_total = kv_parts[-1]
    arrivals = []
    kv_low = []
    for step in reversed(range(planes - 1)):
        with jax.named_scope("kv_back_hop"):
            arrivals.append(line_down(kv_total.astype(BF16)))
        kv_total = arrivals[-1].astype(F32) + kv_parts[step]
        if step:
            kv_total = kv_total.astype(BF16)
            kv_low.append(kv_total)
    with jax.named_scope("kv_back_flip"):
        kv_flipped_total = flip_axis(kv_total[rows:].astype(BF16), "x")
    kv_total = kv_total[:rows] + kv_flipped_total.astype(F32)
    kv_total = kv_total.astype(BF16)
    key_gradient = kv_total[:, :kv_width]
    value_gradient = kv_total[:, kv_width:]

    made_total = None
    for step in reversed(range(STEPS, planes)):
        part = term(made_sums[step // STEPS], step % STEPS)
        with jax.named_scope("made_hop"):
            if made_total is not None:
                part = after(made_total, *OPT['hb'](arrivals)).astype(F32) + part
            made_total = ring_down(part.astype(BF16))
    with jax.named_scope("made0"):
        made_sums[0] = sums(made_backs[0], 0, True, kv_low[0])
    for step in reversed(range(STEPS)):
        moe_sum = made_total.astype(F32) + term(made_sums[0], step)
        if step:
            with jax.named_scope("made_hop"):
                made_total = ring_down(moe_sum.astype(BF16))
    layer_out = (hidden.astype(F32) + moe_sum[:, :width]).astype(BF16)

    found = moe_sum[:, width:].reshape(rows, 4, experts)
    found = found[:, 0] + found[:, 1] + found[:, 2]
    hits = chosen[:, :, None] == jnp.arange(experts, dtype=I32)
    route_dot = jnp.sum(jnp.where(hits, found[:, None, :], 0.0), axis=2)
    share_raw = route_weights[0]
    route_total = jnp.sum(share_raw, axis=1, keepdims=True)
    route_share = share_raw / route_total
    route_gradient = (
        route_dot - jnp.sum(route_share * route_dot, axis=1, keepdims=True)
    ) / route_total
    return (
        layer_out[None],
        residual_gradient[None],
        query_gradient[None],
        key_gradient[None],
        value_gradient[None],
        route_gradient[None],
    )


def solution(mesh):
    fine = Mesh(
        mesh.devices.reshape(mesh.shape["ctx"] // 2, 2, mesh.shape["exp"] // 2, 2),
        ("z", "x", "y", "core"),
    )
    tokens = P(("y", "core"), ("z", "x"), None)
    expert = P(("z", "x", "y", "core"), None, None)
    return jax.shard_map(
        per_device,
        mesh=fine,
        in_specs=(tokens,) * 4 + (P(),) + (tokens,) * 2 + (expert,) * 3 + (tokens,),
        out_specs=(tokens,) * 6,
        check_vma=False,
    )
```
